256 devices in a mesh: samp: 8 (over x, core), var: 32 (over y, z).
Axes of the slice: x: 4, y: 4, z: 8, core: 2. Of those that a mesh axis runs over, the one named last changes fastest.
Arguments:
- samples: bfloat16 [2048, 8192], P('samp', 'var'), may hold values from -12 to 12
- theta_diag: float32 [8192], P('var'), may hold values from 3 to 6
- theta_vals: float32 [2048, 128, 128], P('var'), may hold values from -0.046875 to 0.046875
- theta_cols: int32 [2048, 1], P('var'), may hold values from 0 to 63; in each aligned block of 64 rows (0 to 63, 64 to 127, ...) at most 2 rows name the same one
- theta_count: int32 [64], P('var'), may hold values from 16 to 32
- panel_blocks: int32 [8], replicated, may hold values from 0 to 63, as said below
- act_pan: int32 [256], P('var'), may hold values from 0 to 7, as said below
Outputs:
- inverse: float32 [8192, 1024], P('var', 'samp')
- residual: float32 [8192, 1024], P('var', 'samp')
- gradient: float32 [256, 128, 128], P('var', 'samp')
The draws below stay inside these ranges and needn't reach their ends.
Inputs may be any that keep to these rules, and one draw needn't show every extreme that they name: `theta_cols`: within the slots of one index of var (64 aligned rows), no column block is named more than 2 times. `panel_blocks`: all different. `act_pan`: the 4 entries of one row block are all different.
All inputs are finite; a program needn't handle non-finite values.
Results may differ from the reference program's by a relative error of at most 0.0003.
Values may be sent and summed in bfloat16 or wider, within the bound.
No kernel may reach another device: no remote copies, remote signals or barrier semaphores. Data moves between devices by JAX's collectives and lax.ppermute only.
A program may use at most 128 MiB of HBM per device.

```python
import math
import jax
import jax.numpy as jnp
import numpy as np
from jax import lax

BLK = 128
BLK_DEV = 2
SLOTS = 32
ACTS = 4
CG_STEPS = 2
MOST = 2
NB = 64
NVAR = 8192
PAN_TOT = 8
SAMPLES = 2048


def draw_theta_count(key, part):
    key = jax.random.fold_in(key, 11)
    first_key, second_key = jax.random.split(key)
    counts = jax.random.randint(first_key, (NB,), SLOTS // 2, SLOTS + 1)
    position = jax.random.randint(second_key, (), 0, NB)
    return counts.at[position].set(SLOTS).astype(jnp.int32)


def draw_panel_blocks(key, part):
    key = jax.random.fold_in(key, 23)
    first_key, second_key = jax.random.split(key)
    middle = 1 + jax.random.permutation(first_key, NB - 2)[:PAN_TOT - 2]
    ends = jnp.array([0, NB - 1], dtype=jnp.int32)
    joined = jnp.concatenate([ends, middle.astype(jnp.int32)])
    return jax.random.permutation(second_key, joined).astype(jnp.int32)


def draw_act_pan(key, part):
    key = jax.random.fold_in(key, 37)
    row_keys = jax.random.split(key, NB)
    chosen = jax.vmap(lambda one_key: jax.random.permutation(one_key, PAN_TOT)[:ACTS])(row_keys)
    return chosen.reshape(NB * ACTS).astype(jnp.int32)


def block_scale(key, dims, shards, low, largest):
    factor_of = 1.0
    for dim, shards_of in shards:
        draws = jax.random.uniform(jax.random.fold_in(jax.random.fold_in(key, 6), dim), (shards_of,), jnp.float32, low / len(shards), largest / len(shards))
        factor_of = factor_of * jnp.repeat(jnp.exp(draws), dims[dim] // shards_of).reshape((-1,) + (1,) * (len(dims) - 1 - dim))
    return factor_of


def assign_block(own_key, own, number, rows, number_of, top, reach, lean):
    order = jax.random.permutation(own_key, number_of)
    crowded, usual = load_shares(number_of, rows * top, reach, lean, True), load_shares(number_of, rows * top, reach, lean, False)
    places = jnp.arange(number_of)

    def named(lengths, offset_by):
        used = int((lengths > 0).sum())
        fixed = max(1, used // 4)
        passed = fixed + (places - fixed + offset_by * (used - fixed)) % max(1, number_of - fixed)
        return jnp.zeros((number_of,), jnp.int32).at[order[jnp.where(places < fixed, places, passed)]].set(jnp.asarray(lengths, jnp.int32))

    lengths = jnp.where(number % 4 == 0, named(crowded, number // 4), named(usual, number - number // 4 - 1))
    mixed = jax.random.permutation(jax.random.fold_in(own, 3), number_of)
    donor, receiver = mixed[0:number_of // 2 * 2:2], mixed[1:number_of // 2 * 2:2]
    margin = jnp.minimum(lengths[donor] - 1, reach - lengths[receiver]) // 2
    margin = jnp.where((donor == order[0]) | (receiver == order[0]) | (lengths[receiver] == 0), 0, jnp.maximum(margin, 0))
    passed = jax.random.randint(jax.random.fold_in(own, 4), (number_of // 2,), 0, 1 << 20) % (margin + 1)
    lengths = lengths.at[donor].add(-passed).at[receiver].add(passed)
    items = jnp.searchsorted(jnp.cumsum(lengths), jnp.arange(rows * top), side="right").astype(jnp.int32)
    table = items.reshape(top, rows).T
    table = table[jax.random.permutation(jax.random.fold_in(own, 1), rows)]
    offset_by = jax.random.randint(jax.random.fold_in(own, 2), (rows, 1), 0, top)
    return jnp.take_along_axis(table, (jnp.arange(top)[None, :] + offset_by) % top, axis=1)


def load_shares(amount, total, limit, skew, full):
    portions = [(1 << 20) // math.isqrt(grade ** skew) + 1 for grade in range(1, amount + 1)]
    largest = limit if full else min(limit, max(-(-total // amount), total * portions[0] // sum(portions)))
    least = 1 if total - largest >= amount - 1 else 0
    given, spare = [largest] + [least] * (amount - 1), total - largest - least * (amount - 1)
    while spare > 0:
        candidates = [i for i in range(1, amount) if given[i] < largest] or [i for i in range(1, amount) if given[i] < limit]
        pool, remaining = sum([portions[i] for i in candidates]), spare
        for i in candidates:
            extra = min(limit - given[i], max(1, remaining * portions[i] // pool), spare)
            given[i] = given[i] + extra
            spare = spare - extra
    return np.array(given)


def centred(rng, shape, spread, bound, shards=(), held_as=jnp.bfloat16):
    values = jax.random.normal(rng, shape, jnp.float32) * spread
    if len(shards) > 0:
        values = block_scale(rng, shape, shards, -0.22, 0.18) * values
    return jnp.clip(values, min=-bound, max=bound).astype(held_as)


def setup_inputs(seed: int = 0) -> dict:
    streams_of = jax.random.split(jax.random.key(seed), 8)
    samples = centred(streams_of[0], (SAMPLES, NVAR), 2.0, 12.0, ((0, 8), (1, 32)))
    theta_diag = jnp.clip(jnp.exp(math.log(6.0) - 0.6931472 * jax.random.uniform(streams_of[1], (NVAR,), jnp.float32) ** block_scale(streams_of[1], (NVAR,), ((0, 32),), -0.2, 0.2)), 3.0, 6.0)
    theta_vals = centred(streams_of[2], (NB * SLOTS, BLK, BLK), (4 * BLK * SLOTS) ** -0.5, 0.046875, ((0, 32),), jnp.float32)
    theta_cols_keys = jax.random.split(jax.random.fold_in(streams_of[3], 1), (NB * SLOTS) // (BLK_DEV * SLOTS))
    theta_cols_turns = jax.random.permutation(jax.random.fold_in(streams_of[3], 3), (NB * SLOTS) // (BLK_DEV * SLOTS))
    theta_cols = jax.vmap(lambda own, number: assign_block(jax.random.fold_in(streams_of[3], 2), own, number, BLK_DEV * SLOTS, NB, 1, MOST, 2))(theta_cols_keys, theta_cols_turns).reshape((NB * SLOTS, 1))
    theta_count = draw_theta_count(jax.random.fold_in(streams_of[7], 71), 0)
    panel_blocks = draw_panel_blocks(jax.random.fold_in(streams_of[7], 71), 0)
    act_pan = draw_act_pan(jax.random.fold_in(streams_of[7], 71), 0)
    return {"samples": samples, "theta_diag": theta_diag, "theta_vals": theta_vals, "theta_cols": theta_cols, "theta_count": theta_count, "panel_blocks": panel_blocks, "act_pan": act_pan}


HIGH = lax.Precision.HIGHEST


def apply_theta(panel_field, theta_diag, weights, columns):
    blocks = panel_field.reshape(NB, BLK, -1)
    picked = blocks[columns]
    forward_part = jnp.einsum("eij,ejc->eic", weights, picked, precision=HIGH)
    forward_part = forward_part.reshape(NB, SLOTS, BLK, -1).sum(axis=1)
    own_blocks = jnp.repeat(blocks, SLOTS, axis=0)
    turned = jnp.einsum("eji,ejc->eic", weights, own_blocks, precision=HIGH)
    transposed_part = jnp.zeros_like(blocks).at[columns].add(turned)
    return theta_diag[:, None] * panel_field + (forward_part + transposed_part).reshape(NVAR, -1)


def reference(samples, theta_diag, theta_vals, theta_cols, theta_count, panel_blocks, act_pan):
    columns = theta_cols[:, 0]
    slot_ids = jnp.arange(NB * SLOTS)
    usable = (slot_ids % SLOTS < jnp.repeat(theta_count, SLOTS)).astype(jnp.float32)
    weights = theta_vals * usable[:, None, None]
    row_ids = jnp.arange(NB)
    panel_hits = (row_ids[:, None] == panel_blocks[None, :]).astype(jnp.float32)
    eye_block = jnp.eye(BLK, dtype=jnp.float32)
    target = (panel_hits[:, None, :, None] * eye_block[None, :, None, :]).reshape(NVAR, PAN_TOT * BLK)
    inverse = jnp.zeros_like(target)
    residual = target
    direction = target
    norm_now = jnp.sum(residual * residual, axis=0)
    for iteration in range(CG_STEPS):
        image_field = apply_theta(direction, theta_diag, weights, columns)
        step_size = norm_now / jnp.sum(direction * image_field, axis=0)
        inverse = inverse + step_size * direction
        residual = residual - step_size * image_field
        norm_next = jnp.sum(residual * residual, axis=0)
        direction = residual + (norm_next / norm_now) * direction
        norm_now = norm_next
    active_rows = jnp.arange(NB * ACTS) // ACTS
    active_cols = panel_blocks[act_pan]
    grid = samples.reshape(SAMPLES, NB, BLK)
    left_cols = grid[:, active_rows].astype(jnp.float32)
    right_cols = grid[:, active_cols].astype(jnp.float32)
    gram_part = jnp.einsum("ska,skb->kab", left_cols, right_cols, precision=HIGH)
    chosen = inverse.reshape(NB, BLK, PAN_TOT, BLK)[active_rows, :, act_pan, :]
    gradient = gram_part / SAMPLES - chosen
    return inverse, residual, gradient
```

```python
import jax
import jax.numpy as jnp
from jax import lax
from jax.sharding import PartitionSpec as P

BLK = 128
BLK_DEV = 2
SLOTS = 32
ACTS = 4
HIGH = lax.Precision.HIGHEST
F32 = jnp.float32
BF16 = jnp.bfloat16
YS = 4
ZS = 8


def y_shift(x, k):
    return lax.ppermute(x, "var", [(i, (i + ZS * k) % (YS * ZS)) for i in range(YS * ZS)])


def z_shift(x, k):
    return lax.ppermute(
        x, "var", [(i, (i // ZS) * ZS + (i % ZS + k) % ZS) for i in range(YS * ZS)]
    )


def ring_gather(x):
    h = x.shape[0] // 2
    left, right = y_shift(x, 1), y_shift(x, -1)
    far = [y_shift(left[:h], 1), y_shift(right[h:], -1)]
    block = jnp.concatenate([x, left, right] + far)
    h = block.shape[0] // 2
    parts = [block]
    left = right = block
    for _ in range(3):
        left, right = z_shift(left, 1), z_shift(right, -1)
        parts += [left, right]
    parts += [z_shift(left[:h], 1), z_shift(right[h:], -1)]
    return jnp.concatenate(parts)


def split(v):
    head = lax.reduce_precision(v, 8, 7)
    return head.astype(BF16), (v - head).astype(BF16)


Y_ORDER = (0, -1, 1, 2)
Z_ORDER = (0, -1, 1, -2, 2, -3, 3, 4)


def per_device(samples, theta_diag, theta_vals, theta_cols, theta_count, panel_blocks, act_pan):
    owners = lax.axis_size("var")
    groups = lax.axis_size("samp")
    j = lax.axis_index("var")
    s = lax.axis_index("samp")
    nb = BLK_DEV * owners
    sl = BLK // groups
    rows = BLK_DEV * sl
    size = BLK_DEV * BLK
    pans = groups
    columns = theta_cols[:, 0].reshape(BLK_DEV, SLOTS)
    usable = jnp.arange(SLOTS)[None, :] < theta_count[:, None]
    match = ((columns[:, None, :] == jnp.arange(nb)[None, :, None]) & usable[:, None, :]).astype(F32)

    gathered_x = lax.all_gather(samples, "var", axis=1, tiled=True)

    vals = theta_vals.reshape(BLK_DEV, SLOTS, BLK, BLK)
    row_slice = lax.dynamic_slice_in_dim(vals, s * sl, sl, 2)
    x_local = jnp.einsum("rce,reak->crak", match, row_slice, precision=HIGH)
    got = lax.all_to_all(
        x_local.reshape(owners, BLK_DEV * rows, BLK), "var", 0, 0
    ).reshape(owners, BLK_DEV, BLK_DEV, sl, BLK)

    mine = x_local[panel_blocks]
    from_rows = mine.transpose(1, 2, 0, 3).reshape(rows, pans * BLK)
    picked = got.transpose(0, 2, 1, 3, 4).reshape(nb, BLK_DEV, sl, BLK)[panel_blocks]
    turned = picked.transpose(1, 3, 0, 2).reshape(BLK_DEV, groups, sl, pans * sl)
    turned = turned.transpose(1, 0, 2, 3).reshape(groups, rows, pans * sl)
    turned = lax.all_to_all(turned, "samp", 0, 0)
    from_cols = (
        turned.reshape(groups, rows, pans, sl).transpose(1, 2, 0, 3).reshape(rows, pans * BLK)
    )
    e_slice = from_rows + from_cols
    slice_row = (jnp.arange(BLK_DEV)[:, None] * BLK + s * sl + jnp.arange(sl)[None, :]).reshape(rows)
    global_row = j * size + slice_row
    target_row = (panel_blocks[:, None] * BLK + jnp.arange(BLK)[None, :]).reshape(pans * BLK)
    on_diag = global_row[:, None] == target_row[None, :]
    diag_slice = lax.dynamic_slice_in_dim(theta_diag.reshape(BLK_DEV, BLK), s * sl, sl, 1).reshape(rows)
    u_slice = jnp.where(on_diag, 0.0, e_slice)
    d_part = jnp.sum(jnp.where(on_diag, e_slice + diag_slice[:, None], 0.0), axis=0)
    s2_part = jnp.sum(u_slice * u_slice, axis=0)

    u_all = ring_gather(jnp.concatenate(split(u_slice)))

    col_slice = lax.dynamic_slice_in_dim(vals, s * sl, sl, 3)
    own = jnp.einsum("rce,remk->ckrm", match, col_slice, precision=HIGH)
    a_mat = got.transpose(0, 2, 3, 1, 4).reshape(YS, ZS, rows, size) + own.reshape(
        YS, ZS, rows, size
    )
    y, z = j // ZS, j % ZS
    a_mat = a_mat[(y + jnp.array(Y_ORDER)) % YS]
    a_mat = a_mat[:, (z + jnp.array(Z_ORDER)) % ZS].transpose(1, 0, 2, 3)
    a_hi, a_lo = split(a_mat)

    def doubled(v):
        return jnp.concatenate([v, v], axis=2).reshape(owners * 2 * rows, size)

    def product(v):
        return lax.dot_general(
            doubled(v), u_all, (((0,), (0,)), ((), ())), preferred_element_type=F32
        )

    w_part = product(a_hi) + product(a_lo)

    count_rows = samples.shape[0]
    active_cols = panel_blocks[act_pan]
    left_cols = samples.reshape(count_rows, BLK_DEV, 1, BLK)
    left_cols = jnp.broadcast_to(left_cols, (count_rows, BLK_DEV, ACTS, BLK)).reshape(
        count_rows, BLK_DEV * ACTS, BLK
    )
    right_cols = gathered_x.reshape(count_rows, nb, BLK)[:, active_cols]
    gram_part = jnp.einsum(
        "ska,skb->kab", left_cols, right_cols, preferred_element_type=F32
    )
    gram = lax.psum_scatter(gram_part, "samp", scatter_dimension=1, tiled=True)

    def by_panel(v):
        return v.reshape(-1, pans, BLK).transpose(1, 0, 2)

    scalars = jnp.concatenate([d_part[None], s2_part[None], jnp.zeros((6, pans * BLK), F32)])
    bundle = jnp.concatenate([by_panel(w_part), by_panel(u_slice), by_panel(scalars)], axis=1)
    bundle = lax.all_to_all(bundle, "samp", 0, 0)
    w_sum = jnp.sum(bundle[:, :size], axis=0)
    u = bundle[:, size : size + rows].reshape(groups, BLK_DEV, sl, BLK)
    u = u.transpose(1, 0, 2, 3).reshape(size, BLK)
    ds = jnp.sum(bundle[:, size + rows :], axis=0)
    w = w_sum + theta_diag[:, None] * u
    q_part = jnp.sum(u * w, axis=0)
    tiny = jnp.concatenate([ds[:2], q_part[None], jnp.zeros((5, BLK), F32)])
    tiny = lax.all_to_all(jnp.broadcast_to(tiny[None], (owners, 8, BLK)), "var", 0, 0)
    tiny = jnp.sum(tiny, axis=0)
    d, s2, q = tiny[0], tiny[1], tiny[2]

    alpha1 = 1.0 / d
    rr = s2 * alpha1 * alpha1
    alpha2 = s2 / (q - alpha1 * s2 * s2)
    mine_panel = lax.dynamic_slice_in_dim(panel_blocks, s, 1)
    own_rows = j * size + jnp.arange(size)
    target = (own_rows[:, None] == (mine_panel * BLK + jnp.arange(BLK))[None, :]).astype(F32)
    inverse = (alpha1 + alpha2 * rr) * target - (alpha1 * alpha2) * u
    residual = (alpha1 * alpha2) * w - (alpha1 + alpha2 * rr) * u - (alpha2 * rr * d) * target

    sent = inverse.reshape(BLK_DEV, groups, sl, BLK).transpose(1, 0, 2, 3)
    rows_all = lax.all_to_all(sent.reshape(groups, rows, BLK), "samp", 0, 0)
    rows_all = rows_all.reshape(pans, BLK_DEV, sl, BLK)
    active_rows = jnp.arange(BLK_DEV * ACTS) // ACTS
    chosen = rows_all[act_pan, active_rows]
    gradient = gram * (1.0 / float(count_rows * groups)) - chosen
    return (inverse, residual, gradient)


def solution(mesh):
    in_specs = (
        P("samp", "var"),
        P("var"),
        P("var", None, None),
        P("var", None),
        P("var"),
        P(),
        P("var"),
    )
    out_specs = (P("var", "samp"), P("var", "samp"), P("var", "samp", None))
    return jax.shard_map(
        per_device, mesh=mesh, in_specs=in_specs, out_specs=out_specs, check_vma=False
    )
```

```python
import functools

import jax
import jax.numpy as jnp
from jax import lax
from jax.experimental import pallas as pl
from jax.experimental.pallas import tpu as pltpu
from jax.sharding import PartitionSpec as P

BLK = 128
BLK_DEV = 2
SLOTS = 32
ACTS = 4
F32 = jnp.float32
BF16 = jnp.bfloat16
I16 = jnp.int16
HIGH = lax.Precision.HIGHEST
YS = 4
ZS = 8
OWN = YS * ZS
GRP = 8
SL = BLK // GRP
ROWS = BLK_DEV * SL
SIZE = BLK_DEV * BLK
NB = BLK_DEV * OWN
KACT = BLK_DEV * ACTS
Y_ORDER = (0, -1, 1, 2)
VMEM_LIMIT = 48 * 1024 * 1024
PARAMS = pltpu.CompilerParams(vmem_limit_bytes=VMEM_LIMIT)


def y_shift(x, k):
    return lax.ppermute(x, "var", [(i, (i + ZS * k) % OWN) for i in range(OWN)])


def z_shift(x, k):
    return lax.ppermute(
        x, "var", [(i, (i // ZS) * ZS + (i % ZS + k) % ZS) for i in range(OWN)]
    )


def ring_parts(x):
    block = jnp.concatenate([x, y_shift(x, 1), y_shift(x, -1), y_shift(x, 2)])
    h = block.shape[0] // 2
    parts = [(0, block)]
    left = right = block
    for step in range(1, 4):
        left, right = z_shift(left, 1), z_shift(right, -1)
        parts += [(-step, left), (step, right)]
    parts += [(4, z_shift(left[:h], 1)), (4, z_shift(right[h:], -1))]
    return parts


def whole(shape, dtype):
    return jax.ShapeDtypeStruct(shape, dtype)


def vmem_spec():
    return pl.BlockSpec(memory_space=pltpu.VMEM)


def smem_spec():
    return pl.BlockSpec(memory_space=pltpu.SMEM)


def scale_of(e):
    return jnp.exp2(e.astype(F32) - 15.0)


def code(x, axis):
    most = jnp.max(jnp.abs(x), axis=axis, keepdims=True)
    e = jnp.floor(jnp.log2(jnp.maximum(most, 1e-30))) + 1.0
    q = jnp.floor(x * jnp.exp2(15.0 - e) + 0.5)
    q = jnp.minimum(jnp.maximum(q, -32767.0), 32767.0)
    return q.astype(jnp.int32).astype(I16), e


def value(q):
    return q.astype(jnp.int32).astype(F32)


X_ROWS = BLK_DEV * ROWS
S_ROWS = 16
CHUNK = X_ROWS + S_ROWS + 16


def prep_kernel(meta, v_ref, smp_ref, out_ref, rows_ref, acc, exps):
    acc[...] = jnp.zeros_like(acc)
    exps[...] = jnp.zeros_like(exps)
    for r in range(BLK_DEV):

        def body(e, carry):
            @pl.when(e < meta[1 + r])
            def _():
                c = meta[1 + BLK_DEV + GRP + r * SLOTS + e]
                at = pl.multiple_of((c % BLK_DEV) * ROWS + r * SL, SL)
                acc[c // BLK_DEV, pl.ds(at, SL), :] += v_ref[r * SLOTS + e]

            return carry

        lax.fori_loop(0, SLOTS, body, 0)
    for c in range(BLK_DEV):
        q, e = code(acc[:, c * ROWS : (c + 1) * ROWS, :], 1)
        out_ref[:, c * ROWS : (c + 1) * ROWS, :] = q
        exps[:, c : c + 1, :] = e
    few = S_ROWS // BLK_DEV
    smp = smp_ref[...].astype(F32)
    parts = []
    for c in range(BLK_DEV):
        q, e = code(smp[:, c * few : (c + 1) * few], 1)
        parts.append(value(q))
        exps[:, BLK_DEV + c : BLK_DEV + c + 1, :] = e
    smp = jnp.concatenate(parts, axis=1).astype(jnp.int32)
    out_ref[:, X_ROWS : X_ROWS + S_ROWS, :] = smp.astype(I16)
    out_ref[:, X_ROWS + S_ROWS : CHUNK, :] = exps[...].astype(jnp.int32).astype(I16)
    for p in range(GRP):
        b = meta[1 + BLK_DEV + p]
        at = pl.multiple_of((b % BLK_DEV) * ROWS, ROWS)
        rows_ref[:, p * BLK : (p + 1) * BLK] = acc[b // BLK_DEV, pl.ds(at, ROWS), :]


def prep(meta, theta_vals, smp):
    grid_spec = pltpu.PrefetchScalarGridSpec(
        num_scalar_prefetch=1,
        grid=(1,),
        in_specs=[
            pl.BlockSpec((BLK_DEV * SLOTS, SL, BLK), lambda i, m: (0, m[0], 0)),
            pl.BlockSpec((OWN, S_ROWS, BLK), lambda i, m: (0, 0, 0)),
        ],
        out_specs=[
            pl.BlockSpec((OWN, CHUNK, BLK), lambda i, m: (0, 0, 0)),
            pl.BlockSpec((ROWS, GRP * BLK), lambda i, m: (0, 0)),
        ],
        scratch_shapes=[
            pltpu.VMEM((OWN, X_ROWS, BLK), F32),
            pltpu.VMEM((OWN, 16, BLK), F32),
        ],
    )
    return pl.pallas_call(
        prep_kernel,
        grid_spec=grid_spec,
        out_shape=[whole((OWN, CHUNK, BLK), I16), whole((ROWS, GRP * BLK), F32)],
        compiler_params=PARAMS,
    )(meta, theta_vals, smp)


def pick_kernel(pan, got_ref, out_ref, smp_ref, exp_ref):
    exps = []
    for p in range(GRP):
        e = value(got_ref[pan[p] // BLK_DEV, X_ROWS + S_ROWS : CHUNK, :])
        exps.append(e)
        r = pan[p] % BLK_DEV
        exp_ref[p : p + 1, :] = jnp.where(r == 0, e[2:3], e[3:4])
    for c in range(BLK_DEV):
        stack = []
        for p in range(GRP):
            b = pan[p]
            at = pl.multiple_of(c * ROWS + (b % BLK_DEV) * SL, SL)
            q = value(got_ref[b // BLK_DEV, pl.ds(at, SL), :])
            stack.append(q * scale_of(exps[p][c : c + 1]))
        turned = jnp.concatenate(stack, axis=0).T
        for g in range(GRP):
            out_ref[g, c * SL : (c + 1) * SL, :] = turned[g * SL : (g + 1) * SL]
    few = []
    for p in range(GRP):
        b = pan[p]
        x = value(got_ref[b // BLK_DEV, X_ROWS : X_ROWS + S_ROWS, :])
        few.append(jnp.where(b % BLK_DEV == 0, x[:8], x[8:]))
    smp_ref[...] = jnp.concatenate(few, axis=0)


def pick(pan, got):
    return pl.pallas_call(
        pick_kernel,
        in_specs=[smem_spec(), vmem_spec()],
        out_specs=[vmem_spec()] * 3,
        out_shape=[
            whole((GRP, ROWS, BLK), F32),
            whole((GRP * 8, BLK), F32),
            whole((GRP, BLK), F32),
        ],
        compiler_params=PARAMS,
    )(pan, got)


U_ROWS = GRP * ROWS
F_ROWS = GRP * 8
RING = U_ROWS + F_ROWS + 2 * GRP


def slice_kernel(
    meta, turned_ref, rows_ref, smp_ref, exp_ref, diag_ref, ring_ref, u_ref, d_ref, exps
):
    lane = lax.broadcasted_iota(jnp.int32, (ROWS, BLK), 1)
    row = lax.broadcasted_iota(jnp.int32, (ROWS, BLK), 0)
    in_block = meta[0] * SL + row % SL
    diag = jnp.broadcast_to(diag_ref[...], (ROWS, BLK))
    for p in range(GRP):
        e = rows_ref[:, p * BLK : (p + 1) * BLK]
        for g in range(GRP):
            moved = turned_ref[g]
            if g != p:
                moved = pltpu.roll(moved, ((g - p) * SL) % BLK, 1)
            e = e + jnp.where(lane // SL == g, moved, 0.0)
        hit = (meta[1] * BLK_DEV + row // SL == meta[2 + p]) & (in_block == lane)
        u = jnp.where(hit, 0.0, e)
        u_ref[:, p * BLK : (p + 1) * BLK] = u
        d_ref[p : p + 1, :] = jnp.sum(jnp.where(hit, e + diag, 0.0), axis=0, keepdims=True)
        q, e = code(u, 0)
        ring_ref[p * ROWS : (p + 1) * ROWS, :] = q
        exps[p : p + 1, :] = e
    exps[GRP : 2 * GRP, :] = exp_ref[...]
    ring_ref[U_ROWS : U_ROWS + F_ROWS, :] = smp_ref[...].astype(jnp.int32).astype(I16)
    ring_ref[U_ROWS + F_ROWS :, :] = exps[...].astype(jnp.int32).astype(I16)


def u_slices(meta, turned, from_rows, smp, smp_exp, diag):
    return pl.pallas_call(
        slice_kernel,
        in_specs=[smem_spec()] + [vmem_spec()] * 5,
        out_specs=[vmem_spec()] * 3,
        out_shape=[
            whole((RING, BLK), I16),
            whole((ROWS, GRP * BLK), F32),
            whole((GRP, BLK), F32),
        ],
        scratch_shapes=[pltpu.VMEM((2 * GRP, BLK), F32)],
        compiler_params=PARAMS,
    )(meta, turned, from_rows, smp, smp_exp, diag)


def theta_kernel(meta, got_ref, own_ref, hi_ref, lo_ref):
    for z in range(ZS):
        stack = []
        for dy in Y_ORDER:
            i = ((meta[0] + dy + YS) % YS) * ZS + z
            sc = scale_of(value(got_ref[i, X_ROWS + S_ROWS : CHUNK, :]))
            cols = []
            for c in range(BLK_DEV):
                q = value(got_ref[i, c * ROWS : (c + 1) * ROWS, :])
                cols.append(q * sc[c : c + 1])
            stack.append(jnp.concatenate(cols, axis=1) + own_ref[i])
        x = jnp.concatenate(stack, axis=0).T
        hi = x.astype(BF16)
        lo = (x - hi.astype(F32)).astype(BF16)
        hi_ref[z] = jnp.concatenate([hi, hi], axis=1)
        lo_ref[z] = jnp.concatenate([lo, lo], axis=1)


def theta_parts(meta, got, own):
    return pl.pallas_call(
        theta_kernel,
        in_specs=[smem_spec()] + [vmem_spec()] * 2,
        out_specs=[vmem_spec()] * 2,
        out_shape=[whole((ZS, SIZE, 2 * YS * ROWS), BF16)] * 2,
        compiler_params=PARAMS,
        cost_estimate=pl.CostEstimate(flops=0, bytes_accessed=6_000_000, transcendentals=0),
    )(meta, got, own)


def products(groups, z, a_hi, a_lo, left):
    his, los, fews, lhs_hi, lhs_lo, lhs_few = [], [], [], [], [], []
    for dz, refs in groups:
        zi = (z + dz + ZS) % ZS
        hi, lo = [], []
        for ref in refs:
            for m in range(ref.shape[0] // RING):
                at = m * RING
                sc = scale_of(value(ref[at + U_ROWS + F_ROWS : at + RING, :]))
                u = jnp.concatenate(
                    [
                        value(ref[at + p * ROWS : at + (p + 1) * ROWS, :]) * sc[p : p + 1]
                        for p in range(GRP)
                    ],
                    axis=1,
                )
                head = u.astype(BF16)
                hi.append(head)
                lo.append((u - head.astype(F32)).astype(BF16))
                few = value(ref[at + U_ROWS : at + U_ROWS + F_ROWS, :])
                few = [
                    few[p * 8 : (p + 1) * 8] * sc[GRP + p : GRP + p + 1] for p in range(GRP)
                ]
                fews.append(jnp.concatenate(few, axis=1))
        his += hi + lo
        lhs_hi.append(a_hi[zi])
        lhs_lo.append(a_lo[zi])
        lhs_few.append(left[zi])
    u = jnp.concatenate(his, axis=0)
    w = jnp.dot(jnp.concatenate(lhs_hi, axis=1), u, preferred_element_type=F32)
    w = w + jnp.dot(jnp.concatenate(lhs_lo, axis=1), u, preferred_element_type=F32)
    g = lax.dot_general(
        jnp.concatenate(lhs_few, axis=0).astype(BF16),
        jnp.concatenate(fews, axis=0).astype(BF16),
        (((0,), (0,)), ((), ())),
        preferred_element_type=F32,
    )
    return w, g


BUNDLE = SIZE + KACT * SL + 24


def grouped(shape, refs):
    at, out = 0, []
    for dz, n in shape:
        out.append((dz, refs[at : at + n]))
        at += n
    return out, refs[at:]


def early_kernel(shape, fresh, meta, a_hi, a_lo, left, *refs):
    groups, rest = grouped(shape, refs)
    w, g = products(groups, meta[0], a_hi, a_lo, left)
    if fresh:
        w_ref, g_ref = rest
        w_ref[...], g_ref[...] = w, g
    else:
        w_in, g_in, w_ref, g_ref = rest
        w_ref[...] = w_in[...] + w
        g_ref[...] = g_in[...] + g


def last_kernel(shape, meta, a_hi, a_lo, left, *refs):
    groups, rest = grouped(shape, refs)
    w_in, g_in, u_ref, out_ref, q_ref, s2_ref, g_by = rest
    w_all, g_all = products(groups, meta[0], a_hi, a_lo, left)
    for p in range(GRP):
        cols = slice(p * BLK, (p + 1) * BLK)
        w = w_in[:, cols] + w_all[:, cols]
        u = u_ref[:, cols]
        out_ref[p, 0:SIZE, :] = w
        q_ref[p : p + 1, :] = jnp.sum(u * w, axis=0, keepdims=True)
        s2_ref[p : p + 1, :] = jnp.sum(u * u, axis=0, keepdims=True)
        g_by[p] = g_in[:, cols] + g_all[:, cols]
    for k in range(KACT):
        r = k // ACTS
        mine = g_by[meta[1 + k], r * BLK : (r + 1) * BLK, :]
        for g in range(GRP):
            at = SIZE + k * SL
            out_ref[g, at : at + SL, :] = mine[g * SL : (g + 1) * SL]
    out_ref[:, SIZE + KACT * SL :, :] = jnp.zeros((GRP, 24, BLK), F32)


def flat(groups):
    return tuple((dz, len(refs)) for dz, refs in groups), [r for _, refs in groups for r in refs]


def early_products(meta, theta, left, groups, before):
    shape, refs = flat(groups)
    flops = len(groups) * 2 * 2 * SIZE * SIZE * GRP * BLK
    return pl.pallas_call(
        functools.partial(early_kernel, shape, not before),
        in_specs=[smem_spec()] + [vmem_spec()] * (3 + len(refs) + len(before)),
        out_specs=[vmem_spec()] * 2,
        out_shape=[whole((SIZE, GRP * BLK), F32)] * 2,
        compiler_params=PARAMS,
        cost_estimate=pl.CostEstimate(
            flops=flops, bytes_accessed=len(groups) * 3_000_000, transcendentals=0
        ),
    )(meta, *theta, left, *refs, *before)


def last_products(meta, theta, left, groups, before, u_rows):
    shape, refs = flat(groups)
    return pl.pallas_call(
        functools.partial(last_kernel, shape),
        in_specs=[smem_spec()] + [vmem_spec()] * (6 + len(refs)),
        out_specs=[vmem_spec()] * 3,
        out_shape=[
            whole((GRP, BUNDLE, BLK), F32),
            whole((GRP, BLK), F32),
            whole((GRP, BLK), F32),
        ],
        scratch_shapes=[pltpu.VMEM((GRP, SIZE, BLK), F32)],
        compiler_params=PARAMS,
    )(meta, *theta, left, *refs, *before, u_rows)


def per_device(samples, theta_diag, theta_vals, theta_cols, theta_count, panel_blocks, act_pan):
    j = lax.axis_index("var")
    s = lax.axis_index("samp")
    y, z = j // ZS, j % ZS
    count_rows = samples.shape[0]
    few = count_rows // OWN
    columns = theta_cols[:, 0]

    meta = jnp.concatenate([s[None], theta_count, panel_blocks, columns])
    smp = samples.reshape(OWN, few, BLK_DEV, BLK).transpose(0, 2, 1, 3)
    chunks, from_rows = prep(meta, theta_vals, smp.reshape(OWN, BLK_DEV * few, BLK))
    got = lax.all_to_all(chunks, "var", 0, 0)

    match = (columns.reshape(BLK_DEV, 1, SLOTS) == jnp.arange(NB)[None, :, None]) & (
        jnp.arange(SLOTS)[None, None, :] < theta_count[:, None, None]
    )
    vals = theta_vals.reshape(BLK_DEV, SLOTS, BLK, BLK)
    col_slice = lax.dynamic_slice_in_dim(vals, s * SL, SL, 3)
    own = jnp.einsum("rce,remk->ckrm", match.astype(F32), col_slice, precision=HIGH)
    own = own.reshape(OWN, ROWS, SIZE)
    left = samples.reshape(YS, ZS, few, SIZE)[(y + jnp.array(Y_ORDER)) % YS]
    left = left.transpose(1, 0, 2, 3).reshape(ZS, YS * few, SIZE).astype(F32)
    got, own, left = lax.optimization_barrier((got, own, left))

    turned, few_cols, few_exps = pick(panel_blocks, got)
    turned = lax.all_to_all(turned, "samp", 0, 0)
    diag_slice = lax.dynamic_slice_in_dim(theta_diag.reshape(BLK_DEV, BLK), s * SL, SL, 1)
    diag_slice = diag_slice.reshape(ROWS, 1)
    where = jnp.concatenate([s[None], j[None], panel_blocks])
    ring, u_slice, d_part = u_slices(where, turned, from_rows, few_cols, few_exps, diag_slice)
    parts = ring_parts(ring)

    u_rows = lax.all_to_all(
        jnp.broadcast_to(u_slice[None], (GRP, ROWS, GRP * BLK)), "samp", 0, 0
    )
    u_rows = u_rows.reshape(GRP, BLK_DEV, SL, GRP * BLK).transpose(1, 0, 2, 3)
    u_rows = u_rows.reshape(SIZE, GRP * BLK)

    theta = theta_parts(y[None], got, own)
    where = jnp.concatenate([z[None], act_pan])
    groups = [(dz, [part]) for dz, part in parts[:7]] + [(4, [parts[7][1], parts[8][1]])]
    sums = early_products(where, theta, left, groups[:5], ())
    sums = early_products(where, theta, left, groups[5:7], sums)
    bundle, q_part, s2_part = last_products(where, theta, left, groups[7:], sums, u_rows)

    q_part = q_part + jnp.sum(diag_slice * u_slice * u_slice, axis=0).reshape(GRP, BLK)
    tiny = jnp.concatenate([q_part, d_part, s2_part])
    tiny = lax.all_to_all(jnp.broadcast_to(tiny[None], (OWN, 3 * GRP, BLK)), "var", 0, 0)
    tiny = jnp.sum(tiny, axis=0)
    bundle = bundle.at[:, SIZE + KACT * SL :].set(
        jnp.broadcast_to(tiny[None], (GRP, 3 * GRP, BLK))
    )
    bundle = lax.all_to_all(bundle, "samp", 0, 0)
    total = jnp.sum(bundle, axis=0)
    u = lax.dynamic_slice_in_dim(u_rows, s * BLK, BLK, 1)
    w = total[:SIZE] + theta_diag[:, None] * u
    gram = total[SIZE : SIZE + KACT * SL].reshape(KACT, SL, BLK)
    q = total[SIZE + KACT * SL : SIZE + KACT * SL + GRP]
    d = total[SIZE + KACT * SL + GRP : SIZE + KACT * SL + 2 * GRP]
    s2 = bundle[0, SIZE + KACT * SL + 2 * GRP :]

    alpha1 = 1.0 / d
    rr = s2 * alpha1 * alpha1
    alpha2 = s2 / (q - alpha1 * s2 * s2)
    c_u = alpha1 * alpha2
    c_t = alpha1 + alpha2 * rr
    c_r = alpha2 * rr * d

    def own_panel(v):
        return lax.dynamic_slice_in_dim(v, s, 1, 0)

    mine_panel = lax.dynamic_slice_in_dim(panel_blocks, s, 1)
    own_rows = j * SIZE + jnp.arange(SIZE)
    target = (own_rows[:, None] == (mine_panel * BLK + jnp.arange(BLK))[None, :]).astype(F32)
    inverse = own_panel(c_t) * target - own_panel(c_u) * u
    residual = own_panel(c_u) * w - own_panel(c_t) * u - own_panel(c_r) * target

    slice_row = jnp.arange(BLK_DEV)[:, None] * BLK + s * SL + jnp.arange(SL)[None, :]
    slice_row = j * SIZE + slice_row.reshape(ROWS)
    target_row = (panel_blocks[:, None] * BLK + jnp.arange(BLK)[None, :]).reshape(GRP * BLK)
    on_diag = slice_row[:, None] == target_row[None, :]
    inv_slice = jnp.where(on_diag, c_t.reshape(1, -1), 0.0) - c_u.reshape(1, -1) * u_slice
    inv_slice = inv_slice.reshape(BLK_DEV, SL, GRP, BLK).transpose(2, 0, 1, 3)
    active_rows = jnp.arange(KACT) // ACTS
    gradient = gram * (1.0 / float(count_rows * GRP)) - inv_slice[act_pan, active_rows]
    return (inverse, residual, gradient)


def solution(mesh):
    in_specs = (
        P("samp", "var"),
        P("var"),
        P("var", None, None),
        P("var", None),
        P("var"),
        P(),
        P("var"),
    )
    out_specs = (P("var", "samp"), P("var", "samp"), P("var", "samp", None))
    return jax.shard_map(
        per_device, mesh=mesh, in_specs=in_specs, out_specs=out_specs, check_vma=False
    )
```

```python
import functools

import jax
import jax.numpy as jnp
from jax import lax
from jax.experimental import pallas as pl
from jax.experimental.pallas import tpu as pltpu
from jax.sharding import PartitionSpec as P

BLK = 128
BLK_DEV = 2
SLOTS = 32
ACTS = 4
F32 = jnp.float32
BF16 = jnp.bfloat16
I16 = jnp.int16
HIGH = lax.Precision.HIGHEST
YS = 4
ZS = 8
OWN = YS * ZS
GRP = 8
SL = BLK // GRP
ROWS = BLK_DEV * SL
SIZE = BLK_DEV * BLK
NB = BLK_DEV * OWN
KACT = BLK_DEV * ACTS
Y_ORDER = (0, -1, 1, 2)
PARAMS = pltpu.CompilerParams(vmem_limit_bytes=16 * 1024 * 1024)
WIDE = pltpu.CompilerParams(vmem_limit_bytes=28 * 1024 * 1024)


def y_shift(x, k):
    return lax.ppermute(x, "var", [(i, (i + ZS * k) % OWN) for i in range(OWN)])


def z_shift(x, k):
    return lax.ppermute(
        x, "var", [(i, (i // ZS) * ZS + (i % ZS + k) % ZS) for i in range(OWN)]
    )


def z_across(x):
    pairs = []
    for s in range(GRP):
        for i in range(OWN):
            k = 1 if s % 2 == 0 else -1
            pairs.append((s * OWN + i, s * OWN + (i // ZS) * ZS + (i % ZS + k) % ZS))
    return lax.ppermute(x, ("samp", "var"), pairs)


def whole(shape, dtype):
    return jax.ShapeDtypeStruct(shape, dtype)


def vmem_spec():
    return pl.BlockSpec(memory_space=pltpu.VMEM)


def smem_spec():
    return pl.BlockSpec(memory_space=pltpu.SMEM)


def scale_of(e):
    return jnp.exp2(e.astype(F32) - 15.0)


def code(x, axis):
    most = jnp.max(jnp.abs(x), axis=axis, keepdims=True)
    e = jnp.floor(jnp.log2(jnp.maximum(most, 1e-30))) + 1.0
    q = jnp.floor(x * jnp.exp2(15.0 - e) + 0.5)
    q = jnp.minimum(jnp.maximum(q, -32767.0), 32767.0)
    return q.astype(jnp.int32).astype(I16), e


def value(q):
    return q.astype(jnp.int32).astype(F32)


def spread(diag_ref):
    full = [jnp.broadcast_to(diag_ref[r : r + 1, :], (BLK, BLK)).T for r in range(BLK_DEV)]
    return jnp.concatenate(full, axis=0)


X_ROWS = BLK_DEV * ROWS
S_ROWS = 16
CHUNK = X_ROWS + S_ROWS + 16


def prep_kernel(meta, v_ref, smp_ref, out_ref, rows_ref, acc, exps):
    acc[...] = jnp.zeros_like(acc)
    exps[...] = jnp.zeros_like(exps)
    for r in range(BLK_DEV):

        def body(e, carry):
            @pl.when(e < meta[1 + r])
            def _():
                c = meta[1 + BLK_DEV + GRP + r * SLOTS + e]
                at = pl.multiple_of((c % BLK_DEV) * ROWS + r * SL, SL)
                acc[c // BLK_DEV, pl.ds(at, SL), :] += v_ref[r * SLOTS + e]

            return carry

        lax.fori_loop(0, SLOTS, body, 0)
    for c in range(BLK_DEV):
        q, e = code(acc[:, c * ROWS : (c + 1) * ROWS, :], 1)
        out_ref[:, c * ROWS : (c + 1) * ROWS, :] = q
        exps[:, c : c + 1, :] = e
    few = S_ROWS // BLK_DEV
    smp = smp_ref[...].astype(F32)
    parts = []
    for c in range(BLK_DEV):
        q, e = code(smp[:, c * few : (c + 1) * few], 1)
        parts.append(value(q))
        exps[:, BLK_DEV + c : BLK_DEV + c + 1, :] = e
    smp = jnp.concatenate(parts, axis=1).astype(jnp.int32)
    out_ref[:, X_ROWS : X_ROWS + S_ROWS, :] = smp.astype(I16)
    out_ref[:, X_ROWS + S_ROWS : CHUNK, :] = exps[...].astype(jnp.int32).astype(I16)
    for p in range(GRP):
        b = meta[1 + BLK_DEV + p]
        at = pl.multiple_of((b % BLK_DEV) * ROWS, ROWS)
        rows_ref[:, p * BLK : (p + 1) * BLK] = acc[b // BLK_DEV, pl.ds(at, ROWS), :]


def prep(meta, theta_vals, smp):
    return pl.pallas_call(
        prep_kernel,
        in_specs=[smem_spec()] + [vmem_spec()] * 2,
        out_specs=[vmem_spec()] * 2,
        out_shape=[whole((OWN, CHUNK, BLK), I16), whole((ROWS, GRP * BLK), F32)],
        scratch_shapes=[
            pltpu.VMEM((OWN, X_ROWS, BLK), F32),
            pltpu.VMEM((OWN, 16, BLK), F32),
        ],
        compiler_params=PARAMS,
    )(meta, theta_vals, smp)


def pick_kernel(pan, got_ref, out_ref, smp_ref, exp_ref):
    exps = []
    for p in range(GRP):
        e = value(got_ref[pan[p] // BLK_DEV, X_ROWS + S_ROWS : CHUNK, :])
        exps.append(e)
        r = pan[p] % BLK_DEV
        exp_ref[p : p + 1, :] = jnp.where(r == 0, e[2:3], e[3:4])
    for c in range(BLK_DEV):
        stack = []
        for p in range(GRP):
            b = pan[p]
            at = pl.multiple_of(c * ROWS + (b % BLK_DEV) * SL, SL)
            q = value(got_ref[b // BLK_DEV, pl.ds(at, SL), :])
            stack.append(q * scale_of(exps[p][c : c + 1]))
        turned = jnp.concatenate(stack, axis=0).T
        for g in range(GRP):
            out_ref[g, c * SL : (c + 1) * SL, :] = turned[g * SL : (g + 1) * SL]
    few = []
    for p in range(GRP):
        b = pan[p]
        x = value(got_ref[b // BLK_DEV, X_ROWS : X_ROWS + S_ROWS, :])
        few.append(jnp.where(b % BLK_DEV == 0, x[:8], x[8:]))
    smp_ref[...] = jnp.concatenate(few, axis=0)


def pick(pan, got):
    return pl.pallas_call(
        pick_kernel,
        in_specs=[smem_spec(), vmem_spec()],
        out_specs=[vmem_spec()] * 3,
        out_shape=[
            whole((GRP, ROWS, BLK), F32),
            whole((GRP * 8, BLK), F32),
            whole((GRP, BLK), F32),
        ],
        compiler_params=PARAMS,
    )(pan, got)


U_ROWS = GRP * ROWS
F_ROWS = GRP * 8
RING = U_ROWS + F_ROWS + 2 * GRP
OWN_ROWS = U_ROWS + 2 * GRP


def slice_kernel(
    meta, turned_ref, rows_ref, smp_ref, exp_ref, ring_ref, e_ref, own_ref, exps, own_exps
):
    lane = lax.broadcasted_iota(jnp.int32, (ROWS, BLK), 1)
    row = lax.broadcasted_iota(jnp.int32, (ROWS, BLK), 0)
    in_block = meta[1] * SL + row % SL
    for p in range(GRP):
        e = rows_ref[:, p * BLK : (p + 1) * BLK]
        for g in range(GRP):
            moved = turned_ref[g]
            if g != p:
                moved = pltpu.roll(moved, ((g - p) * SL) % BLK, 1)
            e = e + jnp.where(lane // SL == g, moved, 0.0)
        e_ref[p] = e
        q, x = code(e, 0)
        own_ref[p * ROWS : (p + 1) * ROWS, :] = q
        own_exps[p : p + 1, :] = x
        hit = (meta[2] * BLK_DEV + row // SL == meta[3 + p]) & (in_block == lane)
        q, e = code(jnp.where(hit, 0.0, e), 0)
        ring_ref[p * ROWS : (p + 1) * ROWS, :] = q
        exps[p : p + 1, :] = e
    own_exps[GRP : 2 * GRP, :] = jnp.zeros((GRP, BLK), F32)
    own_ref[U_ROWS:, :] = own_exps[...].astype(jnp.int32).astype(I16)
    exps[GRP : 2 * GRP, :] = exp_ref[...]
    ring_ref[U_ROWS : U_ROWS + F_ROWS, :] = smp_ref[...].astype(jnp.int32).astype(I16)
    ring_ref[U_ROWS + F_ROWS :, :] = exps[...].astype(jnp.int32).astype(I16)


def u_slices(meta, turned, from_rows, smp, smp_exp):
    return pl.pallas_call(
        slice_kernel,
        in_specs=[smem_spec()] + [vmem_spec()] * 4,
        out_specs=[vmem_spec()] * 3,
        out_shape=[
            whole((RING, BLK), I16),
            whole((GRP, ROWS, BLK), F32),
            whole((OWN_ROWS, BLK), I16),
        ],
        scratch_shapes=[pltpu.VMEM((2 * GRP, BLK), F32)] * 2,
        compiler_params=PARAMS,
    )(meta, turned, from_rows, smp, smp_exp)


def theta_kernel(meta, got_ref, own_ref, hi_ref, lo_ref):
    for z in range(ZS):
        stack = []
        for dy in Y_ORDER:
            i = ((meta[0] + dy + YS) % YS) * ZS + z
            sc = scale_of(value(got_ref[i, X_ROWS + S_ROWS : CHUNK, :]))
            cols = []
            for c in range(BLK_DEV):
                q = value(got_ref[i, c * ROWS : (c + 1) * ROWS, :])
                cols.append(q * sc[c : c + 1])
            stack.append(jnp.concatenate(cols, axis=1) + own_ref[i])
        x = jnp.concatenate(stack, axis=0).T
        hi = x.astype(BF16)
        lo = (x - hi.astype(F32)).astype(BF16)
        hi_ref[z] = jnp.concatenate([hi, hi], axis=1)
        lo_ref[z] = jnp.concatenate([lo, lo], axis=1)


def theta_parts(meta, got, own):
    return pl.pallas_call(
        theta_kernel,
        in_specs=[smem_spec()] + [vmem_spec()] * 2,
        out_specs=[vmem_spec()] * 2,
        out_shape=[whole((ZS, SIZE, 2 * YS * ROWS), BF16)] * 2,
        compiler_params=PARAMS,
        cost_estimate=pl.CostEstimate(flops=0, bytes_accessed=6_000_000, transcendentals=0),
    )(meta, got, own)


def products(groups, mats):
    his, los, fews, lhs_hi, lhs_lo, lhs_few = [], [], [], [], [], []
    for refs, (a_hi, a_lo, left) in zip(groups, mats):
        hi, lo = [], []
        for ref in refs:
            for m in range(ref.shape[0] // RING):
                at = m * RING
                sc = scale_of(value(ref[at + U_ROWS + F_ROWS : at + RING, :]))
                u = jnp.concatenate(
                    [
                        value(ref[at + p * ROWS : at + (p + 1) * ROWS, :]) * sc[p : p + 1]
                        for p in range(GRP)
                    ],
                    axis=1,
                )
                head = u.astype(BF16)
                hi.append(head)
                lo.append((u - head.astype(F32)).astype(BF16))
                few = value(ref[at + U_ROWS : at + U_ROWS + F_ROWS, :])
                few = [
                    few[p * 8 : (p + 1) * 8] * sc[GRP + p : GRP + p + 1] for p in range(GRP)
                ]
                fews.append(jnp.concatenate(few, axis=1))
        his += hi + lo
        lhs_hi.append(a_hi[0])
        lhs_lo.append(a_lo[0])
        lhs_few.append(left[0])
    u = jnp.concatenate(his, axis=0)
    w = jnp.dot(jnp.concatenate(lhs_hi, axis=1), u, preferred_element_type=F32)
    w = w + jnp.dot(jnp.concatenate(lhs_lo, axis=1), u, preferred_element_type=F32)
    g = lax.dot_general(
        jnp.concatenate(lhs_few, axis=0).astype(BF16),
        jnp.concatenate(fews, axis=0).astype(BF16),
        (((0,), (0,)), ((), ())),
        preferred_element_type=F32,
    )
    return w, g


G_ROWS = KACT * SL
E_AT = SIZE + G_ROWS
T_AT = E_AT + 16
BUNDLE = T_AT + 48


def grouped(n, refs):
    groups = [[ref] for ref in refs[:n]]
    mats = [refs[n + 3 * i : n + 3 * i + 3] for i in range(n)]
    return groups, mats, refs[4 * n :]


def early_kernel(n, meta, *refs):
    groups, mats, (w_ref, g_ref) = grouped(n, refs)
    w_ref[...], g_ref[...] = products(groups, mats)


def last_kernel(n, meta, *refs):
    groups, mats, rest = grouped(n, refs)
    w_in, g_in, e_ref, diag_ref, out_ref, tiny_ref, u_ref, g_by, u_by, d_by, s2_by = rest
    w_all, g_all = products(groups, mats)
    lane = lax.broadcasted_iota(jnp.int32, (SIZE, BLK), 1)
    row = lax.broadcasted_iota(jnp.int32, (SIZE, BLK), 0)
    in_block = row % BLK
    block = meta[2] * BLK_DEV + row // BLK
    diag = spread(diag_ref)
    mine = jnp.where(in_block // SL == meta[1], diag, 0.0)
    tail = jnp.zeros((14, BLK), F32)
    exps = []
    e_sc = [scale_of(value(e_ref[g, U_ROWS:OWN_ROWS, :])) for g in range(GRP)]
    for p in range(GRP):
        cols = slice(p * BLK, (p + 1) * BLK)
        w = w_in[:, cols] + w_all[:, cols]
        e = jnp.concatenate(
            [
                value(e_ref[g, p * ROWS + r * SL : p * ROWS + (r + 1) * SL, :]) * e_sc[g][p : p + 1]
                for r in range(BLK_DEV)
                for g in range(GRP)
            ],
            axis=0,
        )
        hit = (block == meta[3 + p]) & (in_block == lane)
        u = jnp.where(hit, 0.0, e)
        u_by[p] = u
        d_by[p : p + 1, :] = jnp.sum(jnp.where(hit, e + diag, 0.0), axis=0, keepdims=True)
        s2_by[p : p + 1, :] = jnp.sum(u * u, axis=0, keepdims=True)
        tiny_ref[p : p + 1, :] = jnp.sum(u * (w + mine * u), axis=0, keepdims=True)
        q, x = code(w, 0)
        out_ref[p, 0:SIZE, :] = q
        exps.append(x)
        g_by[p] = g_in[:, cols] + g_all[:, cols]
    own = meta[1]
    u_ref[...] = u_by[own]
    tiny_ref[GRP : GRP + 1, :] = s2_by[pl.ds(own, 1), :]
    tiny_ref[GRP + 1 : GRP + 2, :] = d_by[pl.ds(own, 1), :]
    tiny_ref[GRP + 2 :, :] = jnp.zeros((GRP - 2, BLK), F32)
    active = []
    for k in range(KACT):
        r = k // ACTS
        active.append(g_by[meta[3 + GRP + k], r * BLK : (r + 1) * BLK, :])
    for g in range(GRP):
        x = jnp.concatenate([v[g * SL : (g + 1) * SL] for v in active], axis=0)
        q, x = code(x, 0)
        out_ref[g, SIZE:E_AT, :] = q
        x = jnp.concatenate([exps[g], x, tail], axis=0)
        out_ref[g, E_AT:T_AT, :] = x.astype(jnp.int32).astype(I16)
    out_ref[:, T_AT:, :] = jnp.zeros((GRP, 48, BLK), I16)


def full_spec(shape):
    return pl.BlockSpec(shape, lambda i, m: (0,) * len(shape))


def z_spec(x, dz):
    return pl.BlockSpec((1,) + x.shape[1:], lambda i, m: ((m[0] + dz + ZS) % ZS, 0, 0))


def grouped_call(kernel, meta, theta, left, groups, extra, out_shape, scratch, flops):
    args, specs = [], []
    for _, part in groups:
        args.append(part)
        specs.append(full_spec(part.shape))
    for dz, _ in groups:
        for x in (*theta, left):
            args.append(x)
            specs.append(z_spec(x, dz))
    for x in extra:
        args.append(x)
        specs.append(full_spec(x.shape))
    grid_spec = pltpu.PrefetchScalarGridSpec(
        num_scalar_prefetch=1,
        grid=(1,),
        in_specs=specs,
        out_specs=[full_spec(x.shape) for x in out_shape],
        scratch_shapes=scratch,
    )
    return pl.pallas_call(
        functools.partial(kernel, len(groups)),
        grid_spec=grid_spec,
        out_shape=out_shape,
        compiler_params=WIDE,
        cost_estimate=pl.CostEstimate(
            flops=flops, bytes_accessed=len(groups) * 3_000_000, transcendentals=0
        ),
    )(meta, *args)


def early_products(meta, theta, left, groups):
    flops = len(groups) * 2 * 2 * SIZE * SIZE * GRP * BLK
    out_shape = [whole((SIZE, GRP * BLK), F32)] * 2
    return grouped_call(early_kernel, meta, theta, left, groups, [], out_shape, [], flops)


def last_products(meta, theta, left, groups, before, e_rows, diag):
    flops = len(groups) * 2 * 2 * SIZE * SIZE * GRP * BLK
    out_shape = [
        whole((GRP, BUNDLE, BLK), I16),
        whole((2 * GRP, BLK), F32),
        whole((SIZE, BLK), F32),
    ]
    scratch = [pltpu.VMEM((GRP, SIZE, BLK), F32)] * 2 + [pltpu.VMEM((GRP, BLK), F32)] * 2
    extra = [*before, e_rows, diag]
    return grouped_call(last_kernel, meta, theta, left, groups, extra, out_shape, scratch, flops)


def scalar_kernel(tiny_ref, out_ref):
    x = tiny_ref[0]
    for i in range(1, OWN):
        x = x + tiny_ref[i]
    e = jnp.floor(jnp.log2(jnp.maximum(jnp.abs(x), 1e-30))) + 2.0
    x = x * jnp.exp2(15.0 - e)
    hi = jnp.floor(x)
    lo = jnp.floor((x - hi) * 32768.0)
    x = jnp.concatenate([hi, lo, e], axis=0)
    out_ref[...] = x.astype(jnp.int32).astype(I16)


def scalar_rows(tiny):
    return pl.pallas_call(
        scalar_kernel,
        in_specs=[vmem_spec()],
        out_specs=vmem_spec(),
        out_shape=whole((48, BLK), I16),
        compiler_params=PARAMS,
    )(tiny)


def finish_kernel(
    count, meta, bundle_ref, u_ref, diag_ref, e_ref, inv_ref, res_ref, grad_ref, ct_ref, cu_ref, cr_ref
):
    w, gram, q, s2, d = 0.0, 0.0, 0.0, [], []
    for g in range(GRP):
        sc = scale_of(value(bundle_ref[g, E_AT:T_AT, :]))
        w = w + value(bundle_ref[g, 0:SIZE, :]) * sc[0:1]
        gram = gram + value(bundle_ref[g, SIZE:E_AT, :]) * sc[1:2]
        x = value(bundle_ref[g, T_AT:BUNDLE, :])
        x = (x[0:16] + x[16:32] * (1.0 / 32768.0)) * scale_of(x[32:48])
        q = q + x[0:GRP]
        s2.append(x[GRP : GRP + 1])
        d.append(x[GRP + 1 : GRP + 2])
    s2 = jnp.concatenate(s2, axis=0)
    d = jnp.concatenate(d, axis=0)
    alpha1 = 1.0 / d
    rr = s2 * alpha1 * alpha1
    alpha2 = s2 / (q - alpha1 * s2 * s2)
    ct_ref[...] = alpha1 + alpha2 * rr
    cu_ref[...] = alpha1 * alpha2
    cr_ref[...] = alpha2 * rr * d

    own = pl.ds(meta[1], 1)
    lane = lax.broadcasted_iota(jnp.int32, (SIZE, BLK), 1)
    row = lax.broadcasted_iota(jnp.int32, (SIZE, BLK), 0)
    hit = (meta[2] * BLK_DEV + row // BLK == meta[3 + meta[1]]) & (row % BLK == lane)
    u = u_ref[...]
    w = w + spread(diag_ref) * u
    c_t, c_u, c_r = ct_ref[own, :], cu_ref[own, :], cr_ref[own, :]
    inv_ref[...] = jnp.where(hit, c_t, 0.0) - c_u * u
    res_ref[...] = c_u * w - c_t * u - jnp.where(hit, c_r, 0.0)

    lane = lax.broadcasted_iota(jnp.int32, (SL, BLK), 1)
    row = lax.broadcasted_iota(jnp.int32, (SL, BLK), 0)
    for k in range(KACT):
        p, r = meta[3 + GRP + k], k // ACTS
        e = e_ref[p, r * SL : (r + 1) * SL, :]
        hit = (meta[2] * BLK_DEV + r == meta[3 + p]) & (meta[1] * SL + row == lane)
        part = jnp.where(hit, ct_ref[pl.ds(p, 1), :], -cu_ref[pl.ds(p, 1), :] * e)
        grad_ref[k] = gram[k * SL : (k + 1) * SL] * (1.0 / count) - part


def finish(count, meta, bundle, u, diag, e_slice):
    return pl.pallas_call(
        functools.partial(finish_kernel, count),
        in_specs=[smem_spec()] + [vmem_spec()] * 4,
        out_specs=[vmem_spec()] * 3,
        out_shape=[
            whole((SIZE, BLK), F32),
            whole((SIZE, BLK), F32),
            whole((KACT, SL, BLK), F32),
        ],
        scratch_shapes=[pltpu.VMEM((GRP, BLK), F32)] * 3,
        compiler_params=PARAMS,
    )(meta, bundle, u, diag, e_slice)


def per_device(samples, theta_diag, theta_vals, theta_cols, theta_count, panel_blocks, act_pan):
    j = lax.axis_index("var")
    s = lax.axis_index("samp")
    y, z = j // ZS, j % ZS
    count_rows = samples.shape[0]
    few = count_rows // OWN
    columns = theta_cols[:, 0]
    diag = theta_diag.reshape(BLK_DEV, BLK)

    meta = jnp.concatenate([s[None], theta_count, panel_blocks, columns])
    smp = samples.reshape(OWN, few, BLK_DEV, BLK).transpose(0, 2, 1, 3)
    row_slice = lax.dynamic_slice_in_dim(theta_vals, s * SL, SL, 1)
    chunks, from_rows = prep(meta, row_slice, smp.reshape(OWN, BLK_DEV * few, BLK))
    got = lax.all_to_all(chunks, "var", 0, 0)

    match = (columns.reshape(BLK_DEV, 1, SLOTS) == jnp.arange(NB)[None, :, None]) & (
        jnp.arange(SLOTS)[None, None, :] < theta_count[:, None, None]
    )
    vals = theta_vals.reshape(BLK_DEV, SLOTS, BLK, BLK)
    col_slice = lax.dynamic_slice_in_dim(vals, s * SL, SL, 3)
    own = jnp.einsum("rce,remk->ckrm", match.astype(F32), col_slice, precision=HIGH)
    own = own.reshape(OWN, ROWS, SIZE)
    left = samples.reshape(YS, ZS, few, SIZE)[(y + jnp.array(Y_ORDER)) % YS]
    left = left.transpose(1, 0, 2, 3).reshape(ZS, YS * few, SIZE).astype(F32)
    got, own, left = lax.optimization_barrier((got, own, left))

    turned, few_cols, few_exps = pick(panel_blocks, got)
    turned = lax.all_to_all(turned, "samp", 0, 0)
    place = jnp.concatenate([z[None], s[None], j[None], panel_blocks, act_pan])
    ring, e_slice, e_sent = u_slices(place, turned, from_rows, few_cols, few_exps)

    e_rows = lax.all_to_all(jnp.broadcast_to(e_sent[None], (GRP, OWN_ROWS, BLK)), "samp", 0, 0)

    block = jnp.concatenate([ring, y_shift(ring, 1), y_shift(ring, -1), y_shift(ring, 2)])
    groups = [(0, block)]
    down = up = block
    for step in range(1, 4):
        if step == 3:
            down, up, e_rows = lax.optimization_barrier((down, up, e_rows))
        down, up = z_shift(down, 1), z_shift(up, -1)
        groups += [(-step, down), (step, up)]

    theta = theta_parts(y[None], got, own)
    sums = early_products(place, theta, left, groups[:5])
    across = z_across(jnp.where(s % 2 == 0, down, up))
    groups = [(-3, down), (3, up), (4, across)]
    bundle, tiny, u = last_products(place, theta, left, groups, sums, e_rows, diag)

    tiny = lax.all_to_all(jnp.broadcast_to(tiny[None], (OWN, 2 * GRP, BLK)), "var", 0, 0)
    tiny = scalar_rows(tiny)
    bundle = bundle.at[:, T_AT:].set(jnp.broadcast_to(tiny[None], (GRP, 48, BLK)))
    bundle = lax.all_to_all(bundle, "samp", 0, 0)
    return tuple(finish(float(count_rows * GRP), place, bundle, u, diag, e_slice))


def solution(mesh):
    in_specs = (
        P("samp", "var"),
        P("var"),
        P("var", None, None),
        P("var", None),
        P("var"),
        P(),
        P("var"),
    )
    out_specs = (P("var", "samp"), P("var", "samp"), P("var", "samp", None))
    return jax.shard_map(
        per_device, mesh=mesh, in_specs=in_specs, out_specs=out_specs, check_vma=False
    )
```

```python
import functools

import jax
import jax.numpy as jnp
from jax import lax
from jax.experimental import pallas as pl
from jax.experimental.pallas import tpu as pltpu
from jax.sharding import PartitionSpec as P

BLK = 128
BLK_DEV = 2
SLOTS = 32
ACTS = 4
F32 = jnp.float32
BF16 = jnp.bfloat16
I16 = jnp.int16
HIGH = lax.Precision.HIGHEST
YS = 4
ZS = 8
OWN = YS * ZS
GRP = 8
SL = BLK // GRP
ROWS = BLK_DEV * SL
SIZE = BLK_DEV * BLK
NB = BLK_DEV * OWN
KACT = BLK_DEV * ACTS
CORES = 2
Y_ORDER = (0, -1, 1, 2)
PARAMS = pltpu.CompilerParams(vmem_limit_bytes=16 * 1024 * 1024)
WIDE = pltpu.CompilerParams(vmem_limit_bytes=28 * 1024 * 1024)


def y_shift(x, k):
    return lax.ppermute(x, "var", [(i, (i + ZS * k) % OWN) for i in range(OWN)])


def z_shift(x, k):
    return lax.ppermute(
        x, "var", [(i, (i // ZS) * ZS + (i % ZS + k) % ZS) for i in range(OWN)]
    )


def core_swap(x):
    return lax.ppermute(x, "samp", [(i, i ^ 1) for i in range(GRP)])


def z_across(x):
    pairs = []
    for s in range(GRP):
        for i in range(OWN):
            k = 1 if s % 2 == 0 else -1
            pairs.append((s * OWN + i, s * OWN + (i // ZS) * ZS + (i % ZS + k) % ZS))
    return lax.ppermute(x, ("samp", "var"), pairs)


def whole(shape, dtype):
    return jax.ShapeDtypeStruct(shape, dtype)


def vmem_spec():
    return pl.BlockSpec(memory_space=pltpu.VMEM)


def smem_spec():
    return pl.BlockSpec(memory_space=pltpu.SMEM)


def scale_of(e):
    return jnp.exp2(e.astype(F32) - 15.0)


def code(x, axis):
    most = jnp.max(jnp.abs(x), axis=axis, keepdims=True)
    e = jnp.floor(jnp.log2(jnp.maximum(most, 1e-30))) + 1.0
    q = jnp.floor(x * jnp.exp2(15.0 - e) + 0.5)
    q = jnp.minimum(jnp.maximum(q, -32767.0), 32767.0)
    return q.astype(jnp.int32).astype(I16), e


def value(q):
    return q.astype(jnp.int32).astype(F32)


def spread(diag_ref):
    full = [jnp.broadcast_to(diag_ref[r : r + 1, :], (BLK, BLK)).T for r in range(BLK_DEV)]
    return jnp.concatenate(full, axis=0)


X_ROWS = BLK_DEV * ROWS
S_ROWS = 16
CHUNK = X_ROWS + S_ROWS + 16


def prep_kernel(meta, v_ref, smp_ref, out_ref, rows_ref, acc, exps):
    acc[...] = jnp.zeros_like(acc)
    exps[...] = jnp.zeros_like(exps)
    for r in range(BLK_DEV):

        def body(e, carry):
            @pl.when(e < meta[1 + r])
            def _():
                c = meta[1 + BLK_DEV + GRP + r * SLOTS + e]
                at = pl.multiple_of((c % BLK_DEV) * ROWS + r * SL, SL)
                acc[c // BLK_DEV, pl.ds(at, SL), :] += v_ref[r * SLOTS + e]

            return carry

        lax.fori_loop(0, SLOTS, body, 0)
    for c in range(BLK_DEV):
        q, e = code(acc[:, c * ROWS : (c + 1) * ROWS, :], 1)
        out_ref[:, c * ROWS : (c + 1) * ROWS, :] = q
        exps[:, c : c + 1, :] = e
    few = S_ROWS // BLK_DEV
    smp = smp_ref[...].astype(F32)
    parts = []
    for c in range(BLK_DEV):
        q, e = code(smp[:, c * few : (c + 1) * few], 1)
        parts.append(value(q))
        exps[:, BLK_DEV + c : BLK_DEV + c + 1, :] = e
    smp = jnp.concatenate(parts, axis=1).astype(jnp.int32)
    out_ref[:, X_ROWS : X_ROWS + S_ROWS, :] = smp.astype(I16)
    out_ref[:, X_ROWS + S_ROWS : CHUNK, :] = exps[...].astype(jnp.int32).astype(I16)
    for p in range(GRP):
        b = meta[1 + BLK_DEV + p]
        at = pl.multiple_of((b % BLK_DEV) * ROWS, ROWS)
        rows_ref[:, p * BLK : (p + 1) * BLK] = acc[b // BLK_DEV, pl.ds(at, ROWS), :]


def prep(meta, theta_vals, smp):
    return pl.pallas_call(
        prep_kernel,
        in_specs=[smem_spec()] + [vmem_spec()] * 2,
        out_specs=[vmem_spec()] * 2,
        out_shape=[whole((OWN, CHUNK, BLK), I16), whole((ROWS, GRP * BLK), F32)],
        scratch_shapes=[
            pltpu.VMEM((OWN, X_ROWS, BLK), F32),
            pltpu.VMEM((OWN, 16, BLK), F32),
        ],
        compiler_params=PARAMS,
    )(meta, theta_vals, smp)


def pick_kernel(pan, got_ref, out_ref, smp_ref, exp_ref):
    exps = []
    for p in range(GRP):
        e = value(got_ref[pan[p] // BLK_DEV, X_ROWS + S_ROWS : CHUNK, :])
        exps.append(e)
        r = pan[p] % BLK_DEV
        exp_ref[p : p + 1, :] = jnp.where(r == 0, e[2:3], e[3:4])
    for c in range(BLK_DEV):
        stack = []
        for p in range(GRP):
            b = pan[p]
            at = pl.multiple_of(c * ROWS + (b % BLK_DEV) * SL, SL)
            q = value(got_ref[b // BLK_DEV, pl.ds(at, SL), :])
            stack.append(q * scale_of(exps[p][c : c + 1]))
        turned = jnp.concatenate(stack, axis=0).T
        for g in range(GRP):
            out_ref[g, c * SL : (c + 1) * SL, :] = turned[g * SL : (g + 1) * SL]
    few = []
    for p in range(GRP):
        b = pan[p]
        x = value(got_ref[b // BLK_DEV, X_ROWS : X_ROWS + S_ROWS, :])
        few.append(jnp.where(b % BLK_DEV == 0, x[:8], x[8:]))
    smp_ref[...] = jnp.concatenate(few, axis=0)


def pick(pan, got):
    return pl.pallas_call(
        pick_kernel,
        in_specs=[smem_spec(), vmem_spec()],
        out_specs=[vmem_spec()] * 3,
        out_shape=[
            whole((GRP, ROWS, BLK), F32),
            whole((GRP * 8, BLK), F32),
            whole((GRP, BLK), F32),
        ],
        compiler_params=PARAMS,
    )(pan, got)


U_ROWS = GRP * ROWS
F_ROWS = GRP * 8
RING = U_ROWS + F_ROWS + 2 * GRP
OWN_ROWS = U_ROWS + 2 * GRP


def slice_kernel(
    meta, turned_ref, rows_ref, smp_ref, exp_ref, ring_ref, e_ref, own_ref, exps, own_exps
):
    lane = lax.broadcasted_iota(jnp.int32, (ROWS, BLK), 1)
    row = lax.broadcasted_iota(jnp.int32, (ROWS, BLK), 0)
    in_block = meta[1] * SL + row % SL
    for p in range(GRP):
        e = rows_ref[:, p * BLK : (p + 1) * BLK]
        for g in range(GRP):
            moved = turned_ref[g]
            if g != p:
                moved = pltpu.roll(moved, ((g - p) * SL) % BLK, 1)
            e = e + jnp.where(lane // SL == g, moved, 0.0)
        e_ref[p] = e
        q, x = code(e, 0)
        own_ref[p * ROWS : (p + 1) * ROWS, :] = q
        own_exps[p : p + 1, :] = x
        hit = (meta[2] * BLK_DEV + row // SL == meta[3 + p]) & (in_block == lane)
        q, e = code(jnp.where(hit, 0.0, e), 0)
        ring_ref[p * ROWS : (p + 1) * ROWS, :] = q
        exps[p : p + 1, :] = e
    own_exps[GRP : 2 * GRP, :] = jnp.zeros((GRP, BLK), F32)
    own_ref[U_ROWS:, :] = own_exps[...].astype(jnp.int32).astype(I16)
    exps[GRP : 2 * GRP, :] = exp_ref[...]
    ring_ref[U_ROWS : U_ROWS + F_ROWS, :] = smp_ref[...].astype(jnp.int32).astype(I16)
    ring_ref[U_ROWS + F_ROWS :, :] = exps[...].astype(jnp.int32).astype(I16)


def u_slices(meta, turned, from_rows, smp, smp_exp):
    return pl.pallas_call(
        slice_kernel,
        in_specs=[smem_spec()] + [vmem_spec()] * 4,
        out_specs=[vmem_spec()] * 3,
        out_shape=[
            whole((RING, BLK), I16),
            whole((GRP, ROWS, BLK), F32),
            whole((OWN_ROWS, BLK), I16),
        ],
        scratch_shapes=[pltpu.VMEM((2 * GRP, BLK), F32)] * 2,
        compiler_params=PARAMS,
    )(meta, turned, from_rows, smp, smp_exp)


def theta_kernel(meta, got_ref, own_ref, hi_ref, lo_ref):
    for z in range(ZS):
        stack = []
        for dy in Y_ORDER:
            i = ((meta[0] + dy + YS) % YS) * ZS + z
            sc = scale_of(value(got_ref[i, X_ROWS + S_ROWS : CHUNK, :]))
            cols = []
            for c in range(BLK_DEV):
                q = value(got_ref[i, c * ROWS : (c + 1) * ROWS, :])
                cols.append(q * sc[c : c + 1])
            stack.append(jnp.concatenate(cols, axis=1) + own_ref[i])
        x = jnp.concatenate(stack, axis=0).T
        hi = x.astype(BF16)
        lo = (x - hi.astype(F32)).astype(BF16)
        hi_ref[z] = jnp.concatenate([hi, hi], axis=1)
        lo_ref[z] = jnp.concatenate([lo, lo], axis=1)


def theta_parts(meta, got, own):
    return pl.pallas_call(
        theta_kernel,
        in_specs=[smem_spec()] + [vmem_spec()] * 2,
        out_specs=[vmem_spec()] * 2,
        out_shape=[whole((ZS, SIZE, 2 * YS * ROWS), BF16)] * 2,
        compiler_params=PARAMS,
        cost_estimate=pl.CostEstimate(flops=0, bytes_accessed=6_000_000, transcendentals=0),
    )(meta, got, own)


def products(groups, mats):
    his, los, fews, lhs_hi, lhs_lo, lhs_few = [], [], [], [], [], []
    for refs, (a_hi, a_lo, left) in zip(groups, mats):
        hi, lo = [], []
        for ref in refs:
            for m in range(ref.shape[0] // RING):
                at = m * RING
                sc = scale_of(value(ref[at + U_ROWS + F_ROWS : at + RING, :]))
                u = jnp.concatenate(
                    [
                        value(ref[at + p * ROWS : at + (p + 1) * ROWS, :]) * sc[p : p + 1]
                        for p in range(GRP)
                    ],
                    axis=1,
                )
                head = u.astype(BF16)
                hi.append(head)
                lo.append((u - head.astype(F32)).astype(BF16))
                few = value(ref[at + U_ROWS : at + U_ROWS + F_ROWS, :])
                few = [
                    few[p * 8 : (p + 1) * 8] * sc[GRP + p : GRP + p + 1] for p in range(GRP)
                ]
                fews.append(jnp.concatenate(few, axis=1))
        his += hi + lo
        lhs_hi.append(a_hi[0])
        lhs_lo.append(a_lo[0])
        lhs_few.append(left[0])
    u = jnp.concatenate(his, axis=0)
    w = jnp.dot(jnp.concatenate(lhs_hi, axis=1), u, preferred_element_type=F32)
    w = w + jnp.dot(jnp.concatenate(lhs_lo, axis=1), u, preferred_element_type=F32)
    g = lax.dot_general(
        jnp.concatenate(lhs_few, axis=0).astype(BF16),
        jnp.concatenate(fews, axis=0).astype(BF16),
        (((0,), (0,)), ((), ())),
        preferred_element_type=F32,
    )
    return w, g


G_ROWS = KACT * SL
E_AT = SIZE + G_ROWS
T_AT = E_AT + 16
BUNDLE = T_AT + 48


def grouped(n, refs):
    groups = [[ref] for ref in refs[:n]]
    mats = [refs[n + 3 * i : n + 3 * i + 3] for i in range(n)]
    return groups, mats, refs[4 * n :]


def early_kernel(n, meta, *refs):
    groups, mats, (w_ref, g_ref) = grouped(n, refs)
    w_ref[...], g_ref[...] = products(groups, mats)


def last_kernel(n, meta, *refs):
    groups, mats, rest = grouped(n, refs)
    w_in, g_in, e_ref, diag_ref, keep_ref, send_ref, tiny_ref, u_ref = rest[:8]
    w_by, g_by, a_by, u_by, d_by, s2_by = rest[8:]
    core = meta[1] % CORES
    w_all, g_all = products(groups, mats)
    lane = lax.broadcasted_iota(jnp.int32, (SIZE, BLK), 1)
    row = lax.broadcasted_iota(jnp.int32, (SIZE, BLK), 0)
    in_block = row % BLK
    block = meta[2] * BLK_DEV + row // BLK
    diag = spread(diag_ref)
    mine = jnp.where(in_block // SL == meta[1], diag, 0.0)
    e_sc = [scale_of(value(e_ref[g, U_ROWS:OWN_ROWS, :])) for g in range(GRP)]
    for p in range(GRP):
        cols = slice(p * BLK, (p + 1) * BLK)
        w = w_in[:, cols] + w_all[:, cols]
        e = jnp.concatenate(
            [
                value(e_ref[g, p * ROWS + r * SL : p * ROWS + (r + 1) * SL, :]) * e_sc[g][p : p + 1]
                for r in range(BLK_DEV)
                for g in range(GRP)
            ],
            axis=0,
        )
        hit = (block == meta[3 + p]) & (in_block == lane)
        u = jnp.where(hit, 0.0, e)
        u_by[p] = u
        d_by[p : p + 1, :] = jnp.sum(jnp.where(hit, e + diag, 0.0), axis=0, keepdims=True)
        s2_by[p : p + 1, :] = jnp.sum(u * u, axis=0, keepdims=True)
        tiny_ref[p : p + 1, :] = jnp.sum(u * (w + mine * u), axis=0, keepdims=True)
        w_by[p] = jnp.where(hit, 0.0, w)
        g_by[p] = g_in[:, cols] + g_all[:, cols]
    own = meta[1]
    u_ref[...] = u_by[own]
    tiny_ref[GRP : GRP + 1, :] = s2_by[pl.ds(own, 1), :]
    tiny_ref[GRP + 1 : GRP + 2, :] = d_by[pl.ds(own, 1), :]
    tiny_ref[GRP + 2 :, :] = jnp.zeros((GRP - 2, BLK), F32)
    active = []
    for k in range(KACT):
        r = k // ACTS
        active.append(g_by[meta[3 + GRP + k], r * BLK : (r + 1) * BLK, :])
    for g in range(GRP):
        x = jnp.concatenate([v[g * SL : (g + 1) * SL] for v in active], axis=0)
        a_by[g] = x

    def part(g):
        return w_by[g], a_by[g]

    for i in range(GRP // CORES):
        w, x = part(CORES * i + core)
        keep_ref[i, 0:SIZE, :] = w
        keep_ref[i, SIZE:E_AT, :] = x
        w, x = part(CORES * i + 1 - core)
        fill(send_ref, i, w, x)


def fill(ref, i, w, gram):
    q, w_exp = code(w, 0)
    ref[i, 0:SIZE, :] = q
    q, g_exp = code(gram, 0)
    ref[i, SIZE:E_AT, :] = q
    x = jnp.concatenate([w_exp, g_exp, jnp.zeros((14, BLK), F32)], axis=0)
    ref[i, E_AT:T_AT, :] = x.astype(jnp.int32).astype(I16)


def full_spec(shape):
    return pl.BlockSpec(shape, lambda i, m: (0,) * len(shape))


def z_spec(x, dz):
    return pl.BlockSpec((1,) + x.shape[1:], lambda i, m: ((m[0] + dz + ZS) % ZS, 0, 0))


def grouped_call(kernel, meta, theta, left, groups, extra, out_shape, scratch, flops):
    args, specs = [], []
    for _, part in groups:
        args.append(part)
        specs.append(full_spec(part.shape))
    for dz, _ in groups:
        for x in (*theta, left):
            args.append(x)
            specs.append(z_spec(x, dz))
    for x in extra:
        args.append(x)
        specs.append(full_spec(x.shape))
    grid_spec = pltpu.PrefetchScalarGridSpec(
        num_scalar_prefetch=1,
        grid=(1,),
        in_specs=specs,
        out_specs=[full_spec(x.shape) for x in out_shape],
        scratch_shapes=scratch,
    )
    return pl.pallas_call(
        functools.partial(kernel, len(groups)),
        grid_spec=grid_spec,
        out_shape=out_shape,
        compiler_params=WIDE,
        cost_estimate=pl.CostEstimate(
            flops=flops, bytes_accessed=len(groups) * 3_000_000, transcendentals=0
        ),
    )(meta, *args)


def early_products(meta, theta, left, groups):
    flops = len(groups) * 2 * 2 * SIZE * SIZE * GRP * BLK
    out_shape = [whole((SIZE, GRP * BLK), F32)] * 2
    return grouped_call(early_kernel, meta, theta, left, groups, [], out_shape, [], flops)


def last_products(meta, theta, left, groups, before, e_rows, diag):
    flops = len(groups) * 2 * 2 * SIZE * SIZE * GRP * BLK
    out_shape = [
        whole((GRP // CORES, E_AT, BLK), F32),
        whole((GRP // CORES, T_AT, BLK), I16),
        whole((2 * GRP, BLK), F32),
        whole((SIZE, BLK), F32),
    ]
    scratch = [
        pltpu.VMEM((GRP, SIZE, BLK), F32),
        pltpu.VMEM((GRP, SIZE, BLK), F32),
        pltpu.VMEM((GRP, G_ROWS, BLK), F32),
        pltpu.VMEM((GRP, SIZE, BLK), F32),
        pltpu.VMEM((GRP, BLK), F32),
        pltpu.VMEM((GRP, BLK), F32),
    ]
    extra = [*before, e_rows, diag]
    return grouped_call(last_kernel, meta, theta, left, groups, extra, out_shape, scratch, flops)


def join_kernel(tiny_ref, keep_ref, got_ref, out_ref):
    x = tiny_ref[0]
    for i in range(1, OWN):
        x = x + tiny_ref[i]
    e = jnp.floor(jnp.log2(jnp.maximum(jnp.abs(x), 1e-30))) + 2.0
    x = x * jnp.exp2(15.0 - e)
    hi = jnp.floor(x)
    lo = jnp.floor((x - hi) * 32768.0)
    x = jnp.concatenate([hi, lo, e], axis=0).astype(jnp.int32).astype(I16)
    for i in range(GRP // CORES):
        sc = scale_of(value(got_ref[i, E_AT:T_AT, :]))
        w = keep_ref[i, 0:SIZE, :] + value(got_ref[i, 0:SIZE, :]) * sc[0:1]
        gram = keep_ref[i, SIZE:E_AT, :] + value(got_ref[i, SIZE:E_AT, :]) * sc[1:2]
        fill(out_ref, i, w, gram)
        out_ref[i, T_AT:BUNDLE, :] = x


def join(tiny, keep, got):
    return pl.pallas_call(
        join_kernel,
        in_specs=[vmem_spec()] * 3,
        out_specs=vmem_spec(),
        out_shape=whole((GRP // CORES, BUNDLE, BLK), I16),
        compiler_params=PARAMS,
    )(tiny, keep, got)


def finish_kernel(
    count, meta, bundle_ref, u_ref, diag_ref, e_ref, inv_ref, res_ref, grad_ref, ct_ref, cu_ref, cr_ref, s2_ref
):
    w, gram, q, s2, d = 0.0, 0.0, 0.0, [], []
    first = meta[1] % CORES == 0
    for g in range(GRP // CORES):
        sc = scale_of(value(bundle_ref[g, E_AT:T_AT, :]))
        w = w + value(bundle_ref[g, 0:SIZE, :]) * sc[0:1]
        gram = gram + value(bundle_ref[g, SIZE:E_AT, :]) * sc[1:2]
        x = value(bundle_ref[g, T_AT:BUNDLE, :])
        x = (x[0:16] + x[16:32] * (1.0 / 32768.0)) * scale_of(x[32:48])
        q = q + x[0:GRP]
        own, other = x[GRP : GRP + 2], x[GRP + 2 : GRP + 4]
        for v in (jnp.where(first, own, other), jnp.where(first, other, own)):
            s2.append(v[0:1])
            d.append(v[1:2])
    s2 = jnp.concatenate(s2, axis=0)
    d = jnp.concatenate(d, axis=0)
    alpha1 = 1.0 / d
    rr = s2 * alpha1 * alpha1
    alpha2 = s2 / (q - alpha1 * s2 * s2)
    ct_ref[...] = alpha1 + alpha2 * rr
    cu_ref[...] = alpha1 * alpha2
    cr_ref[...] = alpha2 * rr * d
    s2_ref[...] = s2

    own = pl.ds(meta[1], 1)
    lane = lax.broadcasted_iota(jnp.int32, (SIZE, BLK), 1)
    row = lax.broadcasted_iota(jnp.int32, (SIZE, BLK), 0)
    hit = (meta[2] * BLK_DEV + row // BLK == meta[3 + meta[1]]) & (row % BLK == lane)
    u = u_ref[...]
    w = jnp.where(hit, s2_ref[own, :], w + spread(diag_ref) * u)
    c_t, c_u, c_r = ct_ref[own, :], cu_ref[own, :], cr_ref[own, :]
    inv_ref[...] = jnp.where(hit, c_t, 0.0) - c_u * u
    res_ref[...] = c_u * w - c_t * u - jnp.where(hit, c_r, 0.0)

    lane = lax.broadcasted_iota(jnp.int32, (SL, BLK), 1)
    row = lax.broadcasted_iota(jnp.int32, (SL, BLK), 0)
    for k in range(KACT):
        p, r = meta[3 + GRP + k], k // ACTS
        e = e_ref[p, r * SL : (r + 1) * SL, :]
        hit = (meta[2] * BLK_DEV + r == meta[3 + p]) & (meta[1] * SL + row == lane)
        part = jnp.where(hit, ct_ref[pl.ds(p, 1), :], -cu_ref[pl.ds(p, 1), :] * e)
        grad_ref[k] = gram[k * SL : (k + 1) * SL] * (1.0 / count) - part


def finish(count, meta, bundle, u, diag, e_slice):
    return pl.pallas_call(
        functools.partial(finish_kernel, count),
        in_specs=[smem_spec()] + [vmem_spec()] * 4,
        out_specs=[vmem_spec()] * 3,
        out_shape=[
            whole((SIZE, BLK), F32),
            whole((SIZE, BLK), F32),
            whole((KACT, SL, BLK), F32),
        ],
        scratch_shapes=[pltpu.VMEM((GRP, BLK), F32)] * 4,
        compiler_params=PARAMS,
    )(meta, bundle, u, diag, e_slice)


def per_device(samples, theta_diag, theta_vals, theta_cols, theta_count, panel_blocks, act_pan):
    j = lax.axis_index("var")
    s = lax.axis_index("samp")
    y, z = j // ZS, j % ZS
    count_rows = samples.shape[0]
    few = count_rows // OWN
    columns = theta_cols[:, 0]
    diag = theta_diag.reshape(BLK_DEV, BLK)

    meta = jnp.concatenate([s[None], theta_count, panel_blocks, columns])
    smp = samples.reshape(OWN, few, BLK_DEV, BLK).transpose(0, 2, 1, 3)
    row_slice = lax.dynamic_slice_in_dim(theta_vals, s * SL, SL, 1)
    chunks, from_rows = prep(meta, row_slice, smp.reshape(OWN, BLK_DEV * few, BLK))
    got = lax.all_to_all(chunks, "var", 0, 0)

    match = (columns.reshape(BLK_DEV, 1, SLOTS) == jnp.arange(NB)[None, :, None]) & (
        jnp.arange(SLOTS)[None, None, :] < theta_count[:, None, None]
    )
    vals = theta_vals.reshape(BLK_DEV, SLOTS, BLK, BLK)
    col_slice = lax.dynamic_slice_in_dim(vals, s * SL, SL, 3)
    own = jnp.einsum("rce,remk->ckrm", match.astype(F32), col_slice, precision=HIGH)
    own = own.reshape(OWN, ROWS, SIZE)
    left = samples.reshape(YS, ZS, few, SIZE)[(y + jnp.array(Y_ORDER)) % YS]
    left = left.transpose(1, 0, 2, 3).reshape(ZS, YS * few, SIZE).astype(F32)
    got, own, left = lax.optimization_barrier((got, own, left))

    turned, few_cols, few_exps = pick(panel_blocks, got)
    turned = lax.all_to_all(turned, "samp", 0, 0)
    place = jnp.concatenate([z[None], s[None], j[None], panel_blocks, act_pan])
    ring, e_slice, e_sent = u_slices(place, turned, from_rows, few_cols, few_exps)

    e_rows = lax.all_to_all(jnp.broadcast_to(e_sent[None], (GRP, OWN_ROWS, BLK)), "samp", 0, 0)

    block = jnp.concatenate([ring, y_shift(ring, 1), y_shift(ring, -1), y_shift(ring, 2)])
    groups = [(0, block)]
    down = up = block
    for step in range(1, 4):
        if step == 3:
            down, up, e_rows = lax.optimization_barrier((down, up, e_rows))
        down, up = z_shift(down, 1), z_shift(up, -1)
        groups += [(-step, down), (step, up)]

    theta = theta_parts(y[None], got, own)
    sums = early_products(place, theta, left, groups[:5])
    across = z_across(jnp.where(s % 2 == 0, down, up))
    groups = [(-3, down), (3, up), (4, across)]
    keep, sent, tiny, u = last_products(place, theta, left, groups, sums, e_rows, diag)

    near = core_swap(tiny)
    other = core_swap(sent)
    tiny = jnp.concatenate(
        [tiny[:GRP] + near[:GRP], tiny[GRP : GRP + 2], near[GRP : GRP + 2], jnp.zeros((4, BLK), F32)]
    )
    tiny = lax.all_to_all(jnp.broadcast_to(tiny[None], (OWN, 2 * GRP, BLK)), "var", 0, 0)
    bundle = join(tiny, keep, other)
    sides = [list(range(c, GRP, CORES)) for c in range(CORES)]
    bundle = lax.all_to_all(bundle, "samp", 0, 0, axis_index_groups=sides)
    return tuple(finish(float(count_rows * GRP), place, bundle, u, diag, e_slice))


def solution(mesh):
    in_specs = (
        P("samp", "var"),
        P("var"),
        P("var", None, None),
        P("var", None),
        P("var"),
        P(),
        P("var"),
    )
    out_specs = (P("var", "samp"), P("var", "samp"), P("var", "samp", None))
    return jax.shard_map(
        per_device, mesh=mesh, in_specs=in_specs, out_specs=out_specs, check_vma=False
    )
```

```python
import functools

import jax
import jax.numpy as jnp
from jax import lax
from jax.experimental import pallas as pl
from jax.experimental.pallas import tpu as pltpu
from jax.sharding import PartitionSpec as P

BLK = 128
BLK_DEV = 2
SLOTS = 32
ACTS = 4
F32 = jnp.float32
BF16 = jnp.bfloat16
I16 = jnp.int16
HIGH = lax.Precision.HIGHEST
YS = 4
ZS = 8
OWN = YS * ZS
GRP = 8
SL = BLK // GRP
ROWS = BLK_DEV * SL
SIZE = BLK_DEV * BLK
NB = BLK_DEV * OWN
KACT = BLK_DEV * ACTS
CORES = 2
Y_ORDER = (0, -1, 1, 2)
PARAMS = pltpu.CompilerParams(vmem_limit_bytes=16 * 1024 * 1024)
WIDE = pltpu.CompilerParams(vmem_limit_bytes=28 * 1024 * 1024)


def y_shift(x, k):
    return lax.ppermute(x, "var", [(i, (i + ZS * k) % OWN) for i in range(OWN)])


def z_shift(x, k):
    return lax.ppermute(
        x, "var", [(i, (i // ZS) * ZS + (i % ZS + k) % ZS) for i in range(OWN)]
    )


def core_swap(x):
    return lax.ppermute(x, "samp", [(i, i ^ 1) for i in range(GRP)])


def z_across(x):
    pairs = []
    for s in range(GRP):
        for i in range(OWN):
            k = 1 if s % 2 == 0 else -1
            pairs.append((s * OWN + i, s * OWN + (i // ZS) * ZS + (i % ZS + k) % ZS))
    return lax.ppermute(x, ("samp", "var"), pairs)


def whole(shape, dtype):
    return jax.ShapeDtypeStruct(shape, dtype)


def vmem_spec():
    return pl.BlockSpec(memory_space=pltpu.VMEM)


def smem_spec():
    return pl.BlockSpec(memory_space=pltpu.SMEM)


def scale_of(e):
    return jnp.exp2(e.astype(F32) - 15.0)


def code(x, axis):
    most = jnp.max(jnp.abs(x), axis=axis, keepdims=True)
    e = jnp.floor(jnp.log2(jnp.maximum(most, 1e-30))) + 1.0
    q = jnp.floor(x * jnp.exp2(15.0 - e) + 0.5)
    q = jnp.minimum(jnp.maximum(q, -32767.0), 32767.0)
    return q.astype(jnp.int32).astype(I16), e


def value(q):
    return q.astype(jnp.int32).astype(F32)


def spread(diag_ref):
    full = [jnp.broadcast_to(diag_ref[r : r + 1, :], (BLK, BLK)).T for r in range(BLK_DEV)]
    return jnp.concatenate(full, axis=0)


X_ROWS = BLK_DEV * ROWS
S_ROWS = 16
CHUNK = X_ROWS + S_ROWS + 16
S_EXP = X_ROWS // SL


def prep_kernel(meta, v_ref, smp_ref, out_ref, rows_ref, acc, exps):
    acc[...] = jnp.zeros_like(acc)
    exps[...] = jnp.zeros_like(exps)
    for r in range(BLK_DEV):

        def body(e, carry):
            @pl.when(e < meta[1 + r])
            def _():
                c = meta[1 + BLK_DEV + GRP + r * SLOTS + e]
                at = pl.multiple_of((c % BLK_DEV) * ROWS + r * SL, SL)
                acc[c // BLK_DEV, pl.ds(at, SL), :] += v_ref[r * SLOTS + e]

            return carry

        lax.fori_loop(0, SLOTS, body, 0)
    for c in range(X_ROWS // SL):
        q, e = code(acc[:, c * SL : (c + 1) * SL, :], 1)
        out_ref[:, c * SL : (c + 1) * SL, :] = q
        exps[:, c : c + 1, :] = e
    few = S_ROWS // BLK_DEV
    smp = smp_ref[...].astype(F32)
    parts = []
    for c in range(BLK_DEV):
        q, e = code(smp[:, c * few : (c + 1) * few], 1)
        parts.append(value(q))
        exps[:, S_EXP + c : S_EXP + c + 1, :] = e
    smp = jnp.concatenate(parts, axis=1).astype(jnp.int32)
    out_ref[:, X_ROWS : X_ROWS + S_ROWS, :] = smp.astype(I16)
    out_ref[:, X_ROWS + S_ROWS : CHUNK, :] = exps[...].astype(jnp.int32).astype(I16)
    for p in range(GRP):
        b = meta[1 + BLK_DEV + p]
        at = pl.multiple_of((b % BLK_DEV) * ROWS, ROWS)
        rows_ref[:, p * BLK : (p + 1) * BLK] = acc[b // BLK_DEV, pl.ds(at, ROWS), :]


def prep(meta, theta_vals, smp):
    return pl.pallas_call(
        prep_kernel,
        in_specs=[smem_spec()] + [vmem_spec()] * 2,
        out_specs=[vmem_spec()] * 2,
        out_shape=[whole((OWN, CHUNK, BLK), I16), whole((ROWS, GRP * BLK), F32)],
        scratch_shapes=[
            pltpu.VMEM((OWN, X_ROWS, BLK), F32),
            pltpu.VMEM((OWN, 16, BLK), F32),
        ],
        compiler_params=PARAMS,
    )(meta, theta_vals, smp)


def pick_kernel(pan, got_ref, out_ref, smp_ref, exp_ref):
    exps = []
    for p in range(GRP):
        e = value(got_ref[pan[p] // BLK_DEV, X_ROWS + S_ROWS : CHUNK, :])
        exps.append(e)
        r = pan[p] % BLK_DEV
        exp_ref[p : p + 1, :] = jnp.where(r == 0, e[S_EXP : S_EXP + 1], e[S_EXP + 1 : S_EXP + 2])
    for c in range(BLK_DEV):
        stack = []
        for p in range(GRP):
            b = pan[p]
            at = pl.multiple_of(c * ROWS + (b % BLK_DEV) * SL, SL)
            q = value(got_ref[b // BLK_DEV, pl.ds(at, SL), :])
            e = exps[p][BLK_DEV * c : BLK_DEV * (c + 1)]
            stack.append(q * scale_of(jnp.where(b % BLK_DEV == 0, e[0:1], e[1:2])))
        turned = jnp.concatenate(stack, axis=0).T
        for g in range(GRP):
            out_ref[g, c * SL : (c + 1) * SL, :] = turned[g * SL : (g + 1) * SL]
    few = []
    for p in range(GRP):
        b = pan[p]
        x = value(got_ref[b // BLK_DEV, X_ROWS : X_ROWS + S_ROWS, :])
        few.append(jnp.where(b % BLK_DEV == 0, x[:8], x[8:]))
    smp_ref[...] = jnp.concatenate(few, axis=0)


def pick(pan, got):
    return pl.pallas_call(
        pick_kernel,
        in_specs=[smem_spec(), vmem_spec()],
        out_specs=[vmem_spec()] * 3,
        out_shape=[
            whole((GRP, ROWS, BLK), F32),
            whole((GRP * 8, BLK), F32),
            whole((GRP, BLK), F32),
        ],
        compiler_params=PARAMS,
    )(pan, got)


U_ROWS = GRP * ROWS
F_ROWS = GRP * 8
RING = U_ROWS + F_ROWS + 2 * GRP
OWN_ROWS = U_ROWS + 2 * GRP


def slice_kernel(
    meta, turned_ref, rows_ref, smp_ref, exp_ref, ring_ref, e_ref, own_ref, exps, own_exps
):
    lane = lax.broadcasted_iota(jnp.int32, (ROWS, BLK), 1)
    row = lax.broadcasted_iota(jnp.int32, (ROWS, BLK), 0)
    in_block = meta[1] * SL + row % SL
    for p in range(GRP):
        e = rows_ref[:, p * BLK : (p + 1) * BLK]
        for g in range(GRP):
            moved = turned_ref[g]
            if g != p:
                moved = pltpu.roll(moved, ((g - p) * SL) % BLK, 1)
            e = e + jnp.where(lane // SL == g, moved, 0.0)
        e_ref[p] = e
        q, x = code(e, 0)
        own_ref[p * ROWS : (p + 1) * ROWS, :] = q
        own_exps[p : p + 1, :] = x
        hit = (meta[2] * BLK_DEV + row // SL == meta[3 + p]) & (in_block == lane)
        q, e = code(jnp.where(hit, 0.0, e), 0)
        ring_ref[p * ROWS : (p + 1) * ROWS, :] = q
        exps[p : p + 1, :] = e
    own_exps[GRP : 2 * GRP, :] = jnp.zeros((GRP, BLK), F32)
    own_ref[U_ROWS:, :] = own_exps[...].astype(jnp.int32).astype(I16)
    exps[GRP : 2 * GRP, :] = exp_ref[...]
    ring_ref[U_ROWS : U_ROWS + F_ROWS, :] = smp_ref[...].astype(jnp.int32).astype(I16)
    ring_ref[U_ROWS + F_ROWS :, :] = exps[...].astype(jnp.int32).astype(I16)


def u_slices(meta, turned, from_rows, smp, smp_exp):
    return pl.pallas_call(
        slice_kernel,
        in_specs=[smem_spec()] + [vmem_spec()] * 4,
        out_specs=[vmem_spec()] * 3,
        out_shape=[
            whole((RING, BLK), I16),
            whole((GRP, ROWS, BLK), F32),
            whole((OWN_ROWS, BLK), I16),
        ],
        scratch_shapes=[pltpu.VMEM((2 * GRP, BLK), F32)] * 2,
        compiler_params=PARAMS,
    )(meta, turned, from_rows, smp, smp_exp)


def theta_kernel(meta, got_ref, own_ref, hi_ref, lo_ref):
    for z in range(ZS):
        stack = []
        for dy in Y_ORDER:
            i = ((meta[0] + dy + YS) % YS) * ZS + z
            sc = scale_of(value(got_ref[i, X_ROWS + S_ROWS : CHUNK, :]))
            cols = []
            for c in range(BLK_DEV):
                part = []
                for k in range(BLK_DEV * c, BLK_DEV * (c + 1)):
                    q = value(got_ref[i, k * SL : (k + 1) * SL, :])
                    part.append(q * sc[k : k + 1])
                cols.append(jnp.concatenate(part, axis=0))
            stack.append(jnp.concatenate(cols, axis=1) + own_ref[i])
        x = jnp.concatenate(stack, axis=0).T
        hi = x.astype(BF16)
        lo = (x - hi.astype(F32)).astype(BF16)
        hi_ref[z] = jnp.concatenate([hi, hi], axis=1)
        lo_ref[z] = jnp.concatenate([lo, lo], axis=1)


def theta_parts(meta, got, own):
    return pl.pallas_call(
        theta_kernel,
        in_specs=[smem_spec()] + [vmem_spec()] * 2,
        out_specs=[vmem_spec()] * 2,
        out_shape=[whole((ZS, SIZE, 2 * YS * ROWS), BF16)] * 2,
        compiler_params=PARAMS,
        cost_estimate=pl.CostEstimate(flops=0, bytes_accessed=6_000_000, transcendentals=0),
    )(meta, got, own)


def products(groups, mats):
    his, los, fews, lhs_hi, lhs_lo, lhs_few = [], [], [], [], [], []
    for refs, (a_hi, a_lo, left) in zip(groups, mats):
        hi, lo = [], []
        for ref in refs:
            for m in range(ref.shape[0] // RING):
                at = m * RING
                sc = scale_of(value(ref[at + U_ROWS + F_ROWS : at + RING, :]))
                u = jnp.concatenate(
                    [
                        value(ref[at + p * ROWS : at + (p + 1) * ROWS, :]) * sc[p : p + 1]
                        for p in range(GRP)
                    ],
                    axis=1,
                )
                head = u.astype(BF16)
                hi.append(head)
                lo.append((u - head.astype(F32)).astype(BF16))
                few = value(ref[at + U_ROWS : at + U_ROWS + F_ROWS, :])
                few = [
                    few[p * 8 : (p + 1) * 8] * sc[GRP + p : GRP + p + 1] for p in range(GRP)
                ]
                fews.append(jnp.concatenate(few, axis=1))
        his += hi + lo
        lhs_hi.append(a_hi[0])
        lhs_lo.append(a_lo[0])
        lhs_few.append(left[0])
    u = jnp.concatenate(his, axis=0)
    w = jnp.dot(jnp.concatenate(lhs_hi, axis=1), u, preferred_element_type=F32)
    w = w + jnp.dot(jnp.concatenate(lhs_lo, axis=1), u, preferred_element_type=F32)
    g = lax.dot_general(
        jnp.concatenate(lhs_few, axis=0).astype(BF16),
        jnp.concatenate(fews, axis=0).astype(BF16),
        (((0,), (0,)), ((), ())),
        preferred_element_type=F32,
    )
    return w, g


G_ROWS = KACT * SL
E_AT = SIZE + G_ROWS
T_AT = E_AT + 16
BUNDLE = T_AT + 48


def grouped(n, refs):
    groups = [[ref] for ref in refs[:n]]
    mats = [refs[n + 3 * i : n + 3 * i + 3] for i in range(n)]
    return groups, mats, refs[4 * n :]


def early_kernel(n, meta, *refs):
    groups, mats, (w_ref, g_ref) = grouped(n, refs)
    w_ref[...], g_ref[...] = products(groups, mats)


def last_kernel(n, meta, *refs):
    groups, mats, rest = grouped(n, refs)
    w_in, g_in, e_ref, diag_ref, keep_ref, send_ref, tiny_ref, u_ref = rest[:8]
    w_by, g_by, a_by, u_by, d_by, s2_by = rest[8:]
    core = meta[1] % CORES
    w_all, g_all = products(groups, mats)
    lane = lax.broadcasted_iota(jnp.int32, (SIZE, BLK), 1)
    row = lax.broadcasted_iota(jnp.int32, (SIZE, BLK), 0)
    in_block = row % BLK
    block = meta[2] * BLK_DEV + row // BLK
    diag = spread(diag_ref)
    mine = jnp.where(in_block // SL == meta[1], diag, 0.0)
    e_sc = [scale_of(value(e_ref[g, U_ROWS:OWN_ROWS, :])) for g in range(GRP)]
    for p in range(GRP):
        cols = slice(p * BLK, (p + 1) * BLK)
        w = w_in[:, cols] + w_all[:, cols]
        e = jnp.concatenate(
            [
                value(e_ref[g, p * ROWS + r * SL : p * ROWS + (r + 1) * SL, :]) * e_sc[g][p : p + 1]
                for r in range(BLK_DEV)
                for g in range(GRP)
            ],
            axis=0,
        )
        hit = (block == meta[3 + p]) & (in_block == lane)
        u = jnp.where(hit, 0.0, e)
        u_by[p] = u
        d_by[p : p + 1, :] = jnp.sum(jnp.where(hit, e + diag, 0.0), axis=0, keepdims=True)
        s2_by[p : p + 1, :] = jnp.sum(u * u, axis=0, keepdims=True)
        tiny_ref[p : p + 1, :] = jnp.sum(u * (w + mine * u), axis=0, keepdims=True)
        w_by[p] = jnp.where(hit, 0.0, w)
        g_by[p] = g_in[:, cols] + g_all[:, cols]
    own = meta[1]
    u_ref[...] = u_by[own]
    tiny_ref[GRP : GRP + 1, :] = s2_by[pl.ds(own, 1), :]
    tiny_ref[GRP + 1 : GRP + 2, :] = d_by[pl.ds(own, 1), :]
    tiny_ref[GRP + 2 :, :] = jnp.zeros((GRP - 2, BLK), F32)
    active = []
    for k in range(KACT):
        r = k // ACTS
        active.append(g_by[meta[3 + GRP + k], r * BLK : (r + 1) * BLK, :])
    for g in range(GRP):
        x = jnp.concatenate([v[g * SL : (g + 1) * SL] for v in active], axis=0)
        a_by[g] = x

    def part(g):
        return w_by[g], a_by[g]

    for i in range(GRP // CORES):
        w, x = part(CORES * i + core)
        keep_ref[i, 0:SIZE, :] = w
        keep_ref[i, SIZE:E_AT, :] = x
        w, x = part(CORES * i + 1 - core)
        fill(send_ref, i, w, x)


def fill(ref, i, w, gram):
    q, w_exp = code(w, 0)
    ref[i, 0:SIZE, :] = q
    q, g_exp = code(gram, 0)
    ref[i, SIZE:E_AT, :] = q
    x = jnp.concatenate([w_exp, g_exp, jnp.zeros((14, BLK), F32)], axis=0)
    ref[i, E_AT:T_AT, :] = x.astype(jnp.int32).astype(I16)


def full_spec(shape):
    return pl.BlockSpec(shape, lambda i, m: (0,) * len(shape))


def z_spec(x, dz):
    return pl.BlockSpec((1,) + x.shape[1:], lambda i, m: ((m[0] + dz + ZS) % ZS, 0, 0))


def grouped_call(kernel, meta, theta, left, groups, extra, out_shape, scratch, flops):
    args, specs = [], []
    for _, part in groups:
        args.append(part)
        specs.append(full_spec(part.shape))
    for dz, _ in groups:
        for x in (*theta, left):
            args.append(x)
            specs.append(z_spec(x, dz))
    for x in extra:
        args.append(x)
        specs.append(full_spec(x.shape))
    grid_spec = pltpu.PrefetchScalarGridSpec(
        num_scalar_prefetch=1,
        grid=(1,),
        in_specs=specs,
        out_specs=[full_spec(x.shape) for x in out_shape],
        scratch_shapes=scratch,
    )
    return pl.pallas_call(
        functools.partial(kernel, len(groups)),
        grid_spec=grid_spec,
        out_shape=out_shape,
        compiler_params=WIDE,
        cost_estimate=pl.CostEstimate(
            flops=flops, bytes_accessed=len(groups) * 3_000_000, transcendentals=0
        ),
    )(meta, *args)


def early_products(meta, theta, left, groups):
    flops = len(groups) * 2 * 2 * SIZE * SIZE * GRP * BLK
    out_shape = [whole((SIZE, GRP * BLK), F32)] * 2
    return grouped_call(early_kernel, meta, theta, left, groups, [], out_shape, [], flops)


def last_products(meta, theta, left, groups, before, e_rows, diag):
    flops = len(groups) * 2 * 2 * SIZE * SIZE * GRP * BLK
    out_shape = [
        whole((GRP // CORES, E_AT, BLK), F32),
        whole((GRP // CORES, T_AT, BLK), I16),
        whole((2 * GRP, BLK), F32),
        whole((SIZE, BLK), F32),
    ]
    scratch = [
        pltpu.VMEM((GRP, SIZE, BLK), F32),
        pltpu.VMEM((GRP, SIZE, BLK), F32),
        pltpu.VMEM((GRP, G_ROWS, BLK), F32),
        pltpu.VMEM((GRP, SIZE, BLK), F32),
        pltpu.VMEM((GRP, BLK), F32),
        pltpu.VMEM((GRP, BLK), F32),
    ]
    extra = [*before, e_rows, diag]
    return grouped_call(last_kernel, meta, theta, left, groups, extra, out_shape, scratch, flops)


def join_kernel(tiny_ref, keep_ref, got_ref, out_ref):
    x = tiny_ref[0]
    for i in range(1, OWN):
        x = x + tiny_ref[i]
    e = jnp.floor(jnp.log2(jnp.maximum(jnp.abs(x), 1e-30))) + 2.0
    x = x * jnp.exp2(15.0 - e)
    hi = jnp.floor(x)
    lo = jnp.floor((x - hi) * 32768.0)
    x = jnp.concatenate([hi, lo, e], axis=0).astype(jnp.int32).astype(I16)
    for i in range(GRP // CORES):
        sc = scale_of(value(got_ref[i, E_AT:T_AT, :]))
        w = keep_ref[i, 0:SIZE, :] + value(got_ref[i, 0:SIZE, :]) * sc[0:1]
        gram = keep_ref[i, SIZE:E_AT, :] + value(got_ref[i, SIZE:E_AT, :]) * sc[1:2]
        fill(out_ref, i, w, gram)
        out_ref[i, T_AT:BUNDLE, :] = x


def join(tiny, keep, got):
    return pl.pallas_call(
        join_kernel,
        in_specs=[vmem_spec()] * 3,
        out_specs=vmem_spec(),
        out_shape=whole((GRP // CORES, BUNDLE, BLK), I16),
        compiler_params=PARAMS,
    )(tiny, keep, got)


def finish_kernel(
    count, meta, bundle_ref, u_ref, diag_ref, e_ref, inv_ref, res_ref, grad_ref, ct_ref, cu_ref, cr_ref, s2_ref
):
    w, gram, q, s2, d = 0.0, 0.0, 0.0, [], []
    first = meta[1] % CORES == 0
    for g in range(GRP // CORES):
        sc = scale_of(value(bundle_ref[g, E_AT:T_AT, :]))
        w = w + value(bundle_ref[g, 0:SIZE, :]) * sc[0:1]
        gram = gram + value(bundle_ref[g, SIZE:E_AT, :]) * sc[1:2]
        x = value(bundle_ref[g, T_AT:BUNDLE, :])
        x = (x[0:16] + x[16:32] * (1.0 / 32768.0)) * scale_of(x[32:48])
        q = q + x[0:GRP]
        own, other = x[GRP : GRP + 2], x[GRP + 2 : GRP + 4]
        for v in (jnp.where(first, own, other), jnp.where(first, other, own)):
            s2.append(v[0:1])
            d.append(v[1:2])
    s2 = jnp.concatenate(s2, axis=0)
    d = jnp.concatenate(d, axis=0)
    alpha1 = 1.0 / d
    rr = s2 * alpha1 * alpha1
    alpha2 = s2 / (q - alpha1 * s2 * s2)
    ct_ref[...] = alpha1 + alpha2 * rr
    cu_ref[...] = alpha1 * alpha2
    cr_ref[...] = alpha2 * rr * d
    s2_ref[...] = s2

    own = pl.ds(meta[1], 1)
    lane = lax.broadcasted_iota(jnp.int32, (SIZE, BLK), 1)
    row = lax.broadcasted_iota(jnp.int32, (SIZE, BLK), 0)
    hit = (meta[2] * BLK_DEV + row // BLK == meta[3 + meta[1]]) & (row % BLK == lane)
    u = u_ref[...]
    w = jnp.where(hit, s2_ref[own, :], w + spread(diag_ref) * u)
    c_t, c_u, c_r = ct_ref[own, :], cu_ref[own, :], cr_ref[own, :]
    inv_ref[...] = jnp.where(hit, c_t, 0.0) - c_u * u
    res_ref[...] = c_u * w - c_t * u - jnp.where(hit, c_r, 0.0)

    lane = lax.broadcasted_iota(jnp.int32, (SL, BLK), 1)
    row = lax.broadcasted_iota(jnp.int32, (SL, BLK), 0)
    for k in range(KACT):
        p, r = meta[3 + GRP + k], k // ACTS
        e = e_ref[p, r * SL : (r + 1) * SL, :]
        hit = (meta[2] * BLK_DEV + r == meta[3 + p]) & (meta[1] * SL + row == lane)
        part = jnp.where(hit, ct_ref[pl.ds(p, 1), :], -cu_ref[pl.ds(p, 1), :] * e)
        grad_ref[k] = gram[k * SL : (k + 1) * SL] * (1.0 / count) - part


def finish(count, meta, bundle, u, diag, e_slice):
    return pl.pallas_call(
        functools.partial(finish_kernel, count),
        in_specs=[smem_spec()] + [vmem_spec()] * 4,
        out_specs=[vmem_spec()] * 3,
        out_shape=[
            whole((SIZE, BLK), F32),
            whole((SIZE, BLK), F32),
            whole((KACT, SL, BLK), F32),
        ],
        scratch_shapes=[pltpu.VMEM((GRP, BLK), F32)] * 4,
        compiler_params=PARAMS,
    )(meta, bundle, u, diag, e_slice)


def per_device(samples, theta_diag, theta_vals, theta_cols, theta_count, panel_blocks, act_pan):
    j = lax.axis_index("var")
    s = lax.axis_index("samp")
    y, z = j // ZS, j % ZS
    count_rows = samples.shape[0]
    few = count_rows // OWN
    columns = theta_cols[:, 0]
    diag = theta_diag.reshape(BLK_DEV, BLK)

    meta = jnp.concatenate([s[None], theta_count, panel_blocks, columns])
    smp = samples.reshape(OWN, few, BLK_DEV, BLK).transpose(0, 2, 1, 3)
    row_slice = lax.dynamic_slice_in_dim(theta_vals, s * SL, SL, 1)
    chunks, from_rows = prep(meta, row_slice, smp.reshape(OWN, BLK_DEV * few, BLK))
    got = lax.all_to_all(chunks, "var", 0, 0)

    match = (columns.reshape(BLK_DEV, 1, SLOTS) == jnp.arange(NB)[None, :, None]) & (
        jnp.arange(SLOTS)[None, None, :] < theta_count[:, None, None]
    )
    vals = theta_vals.reshape(BLK_DEV, SLOTS, BLK, BLK)
    col_slice = lax.dynamic_slice_in_dim(vals, s * SL, SL, 3)
    own = jnp.einsum("rce,remk->ckrm", match.astype(F32), col_slice, precision=HIGH)
    own = own.reshape(OWN, ROWS, SIZE)
    left = samples.reshape(YS, ZS, few, SIZE)[(y + jnp.array(Y_ORDER)) % YS]
    left = left.transpose(1, 0, 2, 3).reshape(ZS, YS * few, SIZE).astype(F32)
    got, own, left = lax.optimization_barrier((got, own, left))

    turned, few_cols, few_exps = pick(panel_blocks, got)
    turned = lax.all_to_all(turned, "samp", 0, 0)
    place = jnp.concatenate([z[None], s[None], j[None], panel_blocks, act_pan])
    ring, e_slice, e_sent = u_slices(place, turned, from_rows, few_cols, few_exps)

    e_rows = lax.all_to_all(jnp.broadcast_to(e_sent[None], (GRP, OWN_ROWS, BLK)), "samp", 0, 0)

    block = jnp.concatenate([ring, y_shift(ring, 1), y_shift(ring, -1), y_shift(ring, 2)])
    groups = [(0, block)]
    down = up = block
    for step in range(1, 4):
        if step == 3:
            down, up, e_rows = lax.optimization_barrier((down, up, e_rows))
        down, up = z_shift(down, 1), z_shift(up, -1)
        groups += [(-step, down), (step, up)]

    theta = theta_parts(y[None], got, own)
    sums = early_products(place, theta, left, groups)
    across = z_across(jnp.where(s % 2 == 0, down, up))
    groups = [(4, across)]
    keep, sent, tiny, u = last_products(place, theta, left, groups, sums, e_rows, diag)

    near = core_swap(tiny)
    other = core_swap(sent)
    tiny = jnp.concatenate(
        [tiny[:GRP] + near[:GRP], tiny[GRP : GRP + 2], near[GRP : GRP + 2], jnp.zeros((4, BLK), F32)]
    )
    tiny = lax.all_to_all(jnp.broadcast_to(tiny[None], (OWN, 2 * GRP, BLK)), "var", 0, 0)
    bundle = join(tiny, keep, other)
    sides = [list(range(c, GRP, CORES)) for c in range(CORES)]
    bundle = lax.all_to_all(bundle, "samp", 0, 0, axis_index_groups=sides)
    return tuple(finish(float(count_rows * GRP), place, bundle, u, diag, e_slice))


def solution(mesh):
    in_specs = (
        P("samp", "var"),
        P("var"),
        P("var", None, None),
        P("var", None),
        P("var"),
        P(),
        P("var"),
    )
    out_specs = (P("var", "samp"), P("var", "samp"), P("var", "samp", None))
    return jax.shard_map(
        per_device, mesh=mesh, in_specs=in_specs, out_specs=out_specs, check_vma=False
    )
```
